512 devices in a mesh: row: 16 (over z, core), col: 8 (over y), depth: 4 (over x).
Axes of the slice: x: 4, y: 8, z: 8, core: 2. Of those that a mesh axis runs over, the one named last changes fastest.
Arguments:
- p_blocks: bfloat16 [256, 32, 128, 128], P('row', ('col', 'depth')), may hold values from -0.8984375 to 0.8984375
- p_cols: int32 [256, 32], P('row', ('col', 'depth')), may hold values from 0 to 255, as said below
Outputs:
- square: bfloat16 [256, 32, 128, 128], P('row', ('col', 'depth'))
The draws below stay inside these ranges and needn't reach their ends.
Inputs may be any that keep to these rules, and one draw needn't show every extreme that they name: p_cols[i, m] is congruent to m modulo 32 and lies in the cyclic range from i - 32 to i + 32 - 1 modulo 256.
All inputs are finite; a program needn't handle non-finite values.
Results may differ from the reference program's by a relative error of at most 0.001.
Values may be sent and summed in bfloat16 or wider, within the bound.
No kernel may reach another device: no remote copies, remote signals or barrier semaphores. Data moves between devices by JAX's collectives and lax.ppermute only.
A program may use at most 128 MiB of HBM per device.

```python
import jax
import jax.numpy as jnp
from jax import lax

BS = 128
NCLS = 32
NB = 256


def draw_p_cols(key, part):
    key = jax.random.fold_in(key, 11)
    choose_upper = jax.random.randint(key, (NB, NCLS), 0, 2).astype(jnp.int32)
    row_index = jnp.arange(NB, dtype=jnp.int32)[:, None]
    slot_index = jnp.arange(NCLS, dtype=jnp.int32)[None, :]
    lowest = row_index - NCLS
    first = lowest + jnp.mod(slot_index - lowest, NCLS)
    return jnp.mod(first + NCLS * choose_upper, NB).astype(jnp.int32)


def block_scale(own_key, dims, split, smallest, largest):
    def one(dim, shards_of):
        draws = jax.random.uniform(jax.random.fold_in(jax.random.fold_in(own_key, 6), dim), (shards_of,), jnp.float32, smallest / len(split), largest / len(split))
        return jnp.repeat(jnp.exp(draws), dims[dim] // shards_of).reshape((-1,) + (1,) * (len(dims) - dim - 1))

    gain = one(*split[0])
    for cut in split[1:]:
        gain = gain * one(*cut)
    return gain


def normal_values(stream_key, dims, deviation, reach, shards=(), held_as=jnp.bfloat16):
    gain = block_scale(stream_key, dims, shards, -0.22, 0.18) if shards else 1.0
    array = jax.random.normal(stream_key, dims, jnp.float32) * deviation * gain
    return jnp.minimum(jnp.maximum(array, -reach), reach).astype(held_as)


def setup_inputs(seed: int = 0) -> dict:
    splits = jax.random.split(jax.random.key(seed), 3)
    return {
        "p_blocks": normal_values(splits[0], (NB, NCLS, BS, BS), 0.15, 0.8984375, ((0, 16), (1, 32))),
        "p_cols": draw_p_cols(jax.random.fold_in(splits[2], 71), 0),
    }


def reference(p_blocks, p_cols):
    def row_product(row_index):
        columns = p_cols[row_index]
        left_blocks = p_blocks[row_index].astype(jnp.float32)
        right_blocks = p_blocks[columns].astype(jnp.float32)
        matches = p_cols[columns] == columns[None, :]
        right_blocks = jnp.where(matches[:, :, None, None], right_blocks, jnp.zeros_like(right_blocks))
        result = jnp.einsum('tab,tmbc->mac', left_blocks, right_blocks)
        return result.astype(jnp.bfloat16)

    return lax.map(row_product, jnp.arange(NB, dtype=jnp.int32))
```

```python
import functools

import jax
import jax.numpy as jnp
from jax import lax
from jax.experimental import pallas as pl
from jax.experimental.pallas import tpu as pltpu
from jax.sharding import PartitionSpec as P

BS = 128
TAIL = 16
STEP = 2
QMAX = 32700.0
TINY = 2.0**-111


def passed_along(block, axis, distance):
    n = lax.axis_size(axis)
    return lax.ppermute(block, axis, [(i, (i + distance) % n) for i in range(n)])


def product_kernel(
    rows, panels, classes, idx_ref, x_ref, *refs
):
    shards = refs[:7]
    half_a, half_b = refs[7:9]
    windows = refs[9 : 9 + panels]
    q_ref, own_ref, held, codes, sems = refs[9 + panels :]
    step = pl.program_id(0)
    n_steps = rows // STEP
    zero_at = panels * classes * 4 * BS
    span = 4 * BS

    @pl.when(step == 0)
    def _():
        copies = []
        for p in range(panels):
            for m in range(classes):
                slot = p * classes + m
                copies.append(
                    pltpu.make_async_copy(
                        windows[p].at[m, pl.ds(0, span)],
                        held.at[pl.ds(slot * span, span)],
                        sems.at[slot],
                    )
                )
                copies[-1].start()
        held[pl.ds(zero_at, BS), :] = jnp.zeros((BS, BS), held.dtype)
        for copy in copies:
            copy.wait()

    x = x_ref[0]
    slots = [lax.rem(x + d, classes) for d in range(classes)]
    first_half = step < n_steps // 2
    for r in range(STEP):
        at = slice(r * BS, (r + 1) * BS)
        row = step * STEP + r
        left = [shard[0, at, :] for shard in shards]
        left.append(jnp.where(first_half, half_a[at, :], half_b[at, :]))
        left = jnp.concatenate(left, axis=1)
        right = []
        for d in range(classes):
            picked = []
            for s in range(8):
                k = idx_ref[(row * 8 + s) * classes + slots[d]]
                picked.append(held[pl.ds(pl.multiple_of(k * BS, BS), BS), :])
            right.append(jnp.concatenate(picked, axis=0))
        right = jnp.concatenate(right, axis=1)
        sums = jnp.dot(left, right, preferred_element_type=jnp.float32)
        own_ref[at, :] = sums[:, :BS]
        for d in range(1, classes):
            part = sums[:, d * BS : (d + 1) * BS]
            top = jnp.max(jnp.max(jnp.abs(part), axis=0, keepdims=True), axis=1, keepdims=True)
            code = jnp.ceil(jnp.log2(jnp.maximum(top, TINY)) * 16.0)
            scaled = part * (jnp.exp2(code * (-1.0 / 16.0)) * QMAX)
            coded = jnp.round(jnp.clip(scaled, -32767.0, 32767.0)).astype(jnp.int32)
            q_ref[slots[d], pl.ds(pl.multiple_of(row * BS, BS), BS), :] = coded.astype(jnp.int16)
            codes[d, pl.ds(row, 1), :] = jnp.broadcast_to(code.astype(jnp.int32), (1, BS))

    @pl.when(step == n_steps - 1)
    def _():
        for d in range(1, classes):
            q_ref[slots[d], pl.ds(rows * BS, TAIL), :] = codes[d].astype(jnp.int16)


def products(idx, x, shards, halves, windows, rows, classes):
    panels = len(windows)
    n_steps = rows // STEP
    half = n_steps // 2
    block = STEP * BS
    total_rows = rows * BS + TAIL
    shard_spec = pl.BlockSpec((1, block, BS), lambda g, i, x: (g // half, g % half, 0))
    grid_spec = pltpu.PrefetchScalarGridSpec(
        num_scalar_prefetch=2,
        grid=(n_steps,),
        in_specs=[shard_spec] * 7
        + [
            pl.BlockSpec((block, BS), lambda g, i, x: (jnp.minimum(g, half - 1), 0)),
            pl.BlockSpec((block, BS), lambda g, i, x: (jnp.maximum(g - half, 0), 0)),
        ]
        + [pl.BlockSpec(memory_space=pl.ANY)] * panels,
        out_specs=[
            pl.BlockSpec((classes, total_rows, BS), lambda g, i, x: (0, 0, 0)),
            pl.BlockSpec((block, BS), lambda g, i, x: (g, 0)),
        ],
        scratch_shapes=[
            pltpu.VMEM(((panels * classes * 4 + 1) * BS, BS), jnp.bfloat16),
            pltpu.VMEM((classes, TAIL, BS), jnp.int32),
            pltpu.SemaphoreType.DMA((panels * classes,)),
        ],
    )
    return pl.pallas_call(
        functools.partial(product_kernel, rows, panels, classes),
        grid_spec=grid_spec,
        out_shape=[
            jax.ShapeDtypeStruct((classes, total_rows, BS), jnp.int16),
            jax.ShapeDtypeStruct((rows * BS, BS), jnp.float32),
        ],
        compiler_params=pltpu.CompilerParams(vmem_limit_bytes=40 * 2**20),
        cost_estimate=pl.CostEstimate(
            flops=2 * rows * 32 * BS**3, bytes_accessed=12 * 2**20, transcendentals=0
        ),
    )(idx, x, *shards, *halves, *windows)


def sum_kernel(block_rows, x_ref, own_ref, *refs):
    out_ref = refs[-1]
    parts, codes = refs[0:3], refs[3:6]
    step = pl.program_id(0)
    scales = [jnp.exp2(c[0].astype(jnp.int32).astype(jnp.float32) * (1.0 / 16.0)) * (1.0 / QMAX) for c in codes]
    n_steps = TAIL // block_rows
    for r in range(block_rows):
        at = slice(r * BS, (r + 1) * BS)
        total = own_ref[at, :]
        for part, scale in zip(parts, scales):
            line = scale[r : r + 1, :]
            for other in range(1, n_steps):
                row = other * block_rows + r
                line = jnp.where(step == other, scale[row : row + 1, :], line)
            total = total + part[0, at, :].astype(jnp.int32).astype(jnp.float32) * line
        out_ref[at, :] = total.astype(jnp.bfloat16)


def summed(x, own, received, rows, classes):
    block_rows = 4
    block = block_rows * BS

    def part_spec(d):
        return pl.BlockSpec((1, block, BS), lambda g, x: (lax.rem(x[0] + d, classes), g, 0))

    def code_spec(d):
        return pl.BlockSpec((1, TAIL, BS), lambda g, x: (lax.rem(x[0] + d, classes), rows * BS // TAIL, 0))

    grid_spec = pltpu.PrefetchScalarGridSpec(
        num_scalar_prefetch=1,
        grid=(rows // block_rows,),
        in_specs=[pl.BlockSpec((block, BS), lambda g, x: (g, 0))]
        + [part_spec(d) for d in (1, 2, 3)]
        + [code_spec(d) for d in (1, 2, 3)],
        out_specs=pl.BlockSpec((block, BS), lambda g, x: (g, 0)),
    )
    return pl.pallas_call(
        functools.partial(sum_kernel, block_rows),
        grid_spec=grid_spec,
        out_shape=jax.ShapeDtypeStruct((rows * BS, BS), jnp.bfloat16),
        compiler_params=pltpu.CompilerParams(vmem_limit_bytes=24 * 2**20),
    )(x, own, *[received] * 6)


def shards(p_blocks, p_cols):
    rows = p_blocks.shape[0]
    classes = lax.axis_size("depth")
    matrix_rows = rows * lax.axis_size("row")
    x = lax.axis_index("depth")
    anchor = lax.axis_index("row") * rows - 2 * rows
    blocks = p_blocks[:, 0]
    cols = p_cols[:, 0]
    tail = jnp.zeros((TAIL, BS), jnp.bfloat16).at[0, :rows].set(cols.astype(jnp.bfloat16))

    own = jnp.concatenate(
        [blocks.reshape(2, rows // 2 * BS, BS), jnp.broadcast_to(tail, (2, TAIL, BS))], axis=1
    )
    down = up = own
    left = [own]
    for _ in range(3):
        down = passed_along(down, "col", 1)
        up = passed_along(up, "col", -1)
        left += [down, up]
    halves = [passed_along(down[0], "col", 1), passed_along(up[1], "col", -1)]

    pieces = blocks.reshape(rows // classes, classes, BS, BS).swapaxes(0, 1)
    pieces = jnp.concatenate(
        [pieces.reshape(classes, rows // classes * BS, BS), jnp.broadcast_to(tail, (classes, TAIL, BS))], axis=1
    )
    middle = lax.all_to_all(pieces, "depth", 0, 0)
    windows = [passed_along(middle, "row", 2), passed_along(middle, "row", 1), middle]
    windows += [passed_along(middle, "row", -1), passed_along(middle, "row", -2)]

    left_cols = jnp.stack([s[0, -TAIL, :rows] for s in left] + [halves[0][-TAIL, :rows]], axis=1).astype(jnp.int32)
    window_cols = jnp.stack([w[:, -TAIL, :rows] for w in windows]).astype(jnp.int32)
    own_cols = window_cols[2].T
    place = jnp.mod(left_cols - anchor, matrix_rows) // classes
    n_places = 5 * rows // classes
    by_place = window_cols.reshape(5, classes, rows // classes, classes)
    by_place = jnp.sum(jnp.where(jnp.arange(classes) == x, by_place, 0), axis=-1)
    by_place = by_place.swapaxes(1, 2).reshape(n_places, classes)
    found = (place[:, :, None, None] == jnp.arange(n_places)[:, None]) & (
        by_place[None, None] == own_cols[:, None, None, :]
    )
    per_panel = rows // classes
    where = (place // per_panel)[:, :, None] * (classes * per_panel) + jnp.arange(classes) * per_panel
    where = where + (place % per_panel)[:, :, None]
    idx = jnp.where(jnp.any(found, axis=2), where, n_places * classes).astype(jnp.int32).reshape(-1)

    x_operand = jnp.reshape(x, (1,)).astype(jnp.int32)
    coded, mine = products(idx, x_operand, left, halves, windows, rows, classes)
    received = lax.all_to_all(coded, "depth", 0, 0)
    total = summed(x_operand, mine, received, rows, classes)
    return total.reshape(rows, 1, BS, BS)


def solution(mesh):
    return jax.shard_map(
        shards,
        mesh=mesh,
        in_specs=(P("row", ("col", "depth"), None, None), P("row", ("col", "depth"))),
        out_specs=P("row", ("col", "depth"), None, None),
        check_vma=False,
    )
```

```python
import functools

import jax
import jax.numpy as jnp
from jax import lax
from jax.experimental import pallas as pl
from jax.experimental.pallas import tpu as pltpu
from jax.sharding import PartitionSpec as P

BS = 128
TAIL = 16
STEP = 4
PANELS = 5
SPAN = 4 * BS + TAIL
QMAX = 32700.0
TINY = 2.0**-111


def passed_along(block, axis, distance):
    n = lax.axis_size(axis)
    return lax.ppermute(block, axis, [(i, (i + distance) % n) for i in range(n)])


def offsets(left_tails, held, x, anchor, matrix_rows, classes, zero_at):
    sub = lax.broadcasted_iota(jnp.int32, (8, BS), 0)
    lane = lax.broadcasted_iota(jnp.int32, (8, BS), 1)

    def numbers(tile):
        return tile.astype(jnp.float32)[:8].astype(jnp.int32)

    cols = jnp.zeros((8, BS), jnp.int32)
    for s in range(8):
        cols = jnp.where(sub == s, numbers(left_tails[s]), cols)
    place = lax.shift_right_logical((cols - anchor + 2 * matrix_rows) & (matrix_rows - 1), 2)
    base = lax.shift_right_logical(place, 2) * (classes * SPAN) + (place & 3) * BS
    result = []
    for m in range(classes):
        tails = [numbers(held[pl.ds((p * classes + m) * SPAN + 4 * BS, TAIL), :]) for p in range(PANELS)]
        found = jnp.zeros((8, BS), jnp.int32)
        for p in range(PANELS):
            for a in range(4):
                column = jnp.sum(jnp.where(lane == 4 * a + x, tails[p], 0), axis=1, keepdims=True)
                hit = (place == 4 * p + a) & (tails[PANELS // 2] == column)
                found = jnp.where(hit, 1, found)
        result.append(jnp.where(found == 1, base + m * SPAN, zero_at))
    return result


def product_kernel(rows, classes, matrix_rows, here_ref, *refs):
    shards = refs[:7]
    half_a, half_b = refs[7:9]
    tail_sources = refs[9:17]
    pair, far, cross = refs[17:20]
    q_ref, own_ref, held, tails, wide, idx_ref, sems = refs[20:]
    step = pl.program_id(0)
    n_steps = rows // STEP
    panel = classes * SPAN
    zero_at = PANELS * panel
    x, core, anchor = here_ref[0], here_ref[1], here_ref[2]

    @pl.when(step == 0)
    def _():
        pieces = [
            (pair.at[pl.ds(0, panel)], 2 - core),
            (pair.at[pl.ds(panel, panel)], 3 - core),
            (far.at[pl.ds(0, panel)], 3 * core),
            (far.at[pl.ds(panel, panel)], 1 + 3 * core),
            (cross, 4 - 4 * core),
        ]
        copies = []
        for n, (source, p) in enumerate(pieces):
            at = pl.ds(pl.multiple_of(p * panel, TAIL), panel)
            copies.append(pltpu.make_async_copy(source, held.at[at], sems.at[n]))
        for s in range(8):
            if s < 7:
                source = tail_sources[s].at[0, pl.ds(rows // 2 * BS, TAIL)]
            else:
                source = tail_sources[s].at[pl.ds(rows // 2 * BS, TAIL)]
            copies.append(pltpu.make_async_copy(source, tails.at[s], sems.at[len(pieces) + s]))
        for copy in copies:
            copy.start()
        held[pl.ds(zero_at, BS), :] = jnp.zeros((BS, BS), held.dtype)
        for copy in copies:
            copy.wait()
        found = offsets([tails[s] for s in range(8)], held, x, anchor, matrix_rows, classes, zero_at)
        for m in range(classes):
            wide[pl.ds(m * 8, 8), :] = found[m]
        copy = pltpu.make_async_copy(wide, idx_ref, sems.at[len(copies)])
        copy.start()
        copy.wait()

    slots = [lax.rem(x + d, classes) for d in range(classes)]
    first_half = step < n_steps // 2
    codes = [[] for _ in range(classes)]
    for r in range(STEP):
        at = slice(r * BS, (r + 1) * BS)
        row = step * STEP + r
        left = [shard[0, at, :] for shard in shards]
        left.append(jnp.where(first_half, half_a[at, :], half_b[at, :]))
        left = jnp.concatenate(left, axis=1)
        right = []
        for d in range(classes):
            picked = []
            for s in range(8):
                k = idx_ref[slots[d] * 8 + s, row]
                picked.append(held[pl.ds(pl.multiple_of(k, TAIL), BS), :])
            right.append(jnp.concatenate(picked, axis=0))
        right = jnp.concatenate(right, axis=1)
        sums = jnp.dot(left, right, preferred_element_type=jnp.float32)
        own_ref[at, :] = sums[:, :BS]
        for d in range(1, classes):
            part = sums[:, d * BS : (d + 1) * BS]
            top = jnp.max(jnp.max(jnp.abs(part), axis=0, keepdims=True), axis=1, keepdims=True)
            code = jnp.ceil(jnp.log2(jnp.maximum(top, TINY)) * 16.0)
            scaled = part * (jnp.exp2(code * (-1.0 / 16.0)) * QMAX)
            coded = jnp.round(jnp.clip(scaled, -32767.0, 32767.0)).astype(jnp.int32)
            q_ref[slots[d], 0, at, :] = coded.astype(jnp.int16)
            codes[d].append(code)
    sub = lax.broadcasted_iota(jnp.int32, (TAIL, BS), 0)
    for d in range(1, classes):
        lines = jnp.zeros((TAIL, BS), jnp.float32)
        for r in range(STEP):
            lines = jnp.where(sub == r, codes[d][r], lines)
        q_ref[slots[d], 0, pl.ds(STEP * BS, TAIL), :] = lines.astype(jnp.int32).astype(jnp.int16)


def products(here, shards, halves, windows, rows, classes, matrix_rows):
    n_steps = rows // STEP
    half = n_steps // 2
    block = STEP * BS
    shard_spec = pl.BlockSpec((1, block, BS), lambda g, h: (g // half, g % half, 0))
    anywhere = pl.BlockSpec(memory_space=pl.ANY)
    grid_spec = pltpu.PrefetchScalarGridSpec(
        num_scalar_prefetch=1,
        grid=(n_steps,),
        in_specs=[shard_spec] * 7
        + [
            pl.BlockSpec((block, BS), lambda g, h: (jnp.minimum(g, half - 1), 0)),
            pl.BlockSpec((block, BS), lambda g, h: (jnp.maximum(g - half, 0), 0)),
        ]
        + [anywhere] * 11,
        out_specs=[
            pl.BlockSpec((classes, 1, block + TAIL, BS), lambda g, h: (0, g, 0, 0)),
            pl.BlockSpec((block, BS), lambda g, h: (g, 0)),
        ],
        scratch_shapes=[
            pltpu.VMEM((PANELS * classes * SPAN + BS, BS), jnp.bfloat16),
            pltpu.VMEM((8, TAIL, BS), jnp.bfloat16),
            pltpu.VMEM((classes * 8, BS), jnp.int32),
            pltpu.SMEM((classes * 8, BS), jnp.int32),
            pltpu.SemaphoreType.DMA((14,)),
        ],
    )
    return pl.pallas_call(
        functools.partial(product_kernel, rows, classes, matrix_rows),
        grid_spec=grid_spec,
        out_shape=[
            jax.ShapeDtypeStruct((classes, n_steps, block + TAIL, BS), jnp.int16),
            jax.ShapeDtypeStruct((rows * BS, BS), jnp.float32),
        ],
        compiler_params=pltpu.CompilerParams(vmem_limit_bytes=24 * 2**20),
        cost_estimate=pl.CostEstimate(
            flops=2 * rows * 32 * BS**3, bytes_accessed=12 * 2**20, transcendentals=0
        ),
    )(here, *shards, *halves, *shards, halves[0], *windows)


def sum_kernel(here_ref, own_ref, *refs):
    out_ref = refs[-1]
    scales = []
    for part in refs[:-1]:
        code = part[0, 0, pl.ds(STEP * BS, TAIL), :].astype(jnp.int32).astype(jnp.float32)
        scales.append(jnp.exp2(code * (1.0 / 16.0)) * (1.0 / QMAX))
    for r in range(STEP):
        at = slice(r * BS, (r + 1) * BS)
        total = own_ref[at, :]
        for part, scale in zip(refs[:-1], scales):
            total = total + part[0, 0, at, :].astype(jnp.int32).astype(jnp.float32) * scale[r : r + 1, :]
        out_ref[at, :] = total.astype(jnp.bfloat16)


def summed(here, own, received, rows, classes):
    block = STEP * BS

    def part_spec(d):
        return pl.BlockSpec((1, 1, block + TAIL, BS), lambda g, h: (lax.rem(h[0] + d, classes), g, 0, 0))

    grid_spec = pltpu.PrefetchScalarGridSpec(
        num_scalar_prefetch=1,
        grid=(rows // STEP,),
        in_specs=[pl.BlockSpec((block, BS), lambda g, h: (g, 0))] + [part_spec(d) for d in (1, 2, 3)],
        out_specs=pl.BlockSpec((block, BS), lambda g, h: (g, 0)),
    )
    return pl.pallas_call(
        sum_kernel,
        grid_spec=grid_spec,
        out_shape=jax.ShapeDtypeStruct((rows * BS, BS), jnp.bfloat16),
        compiler_params=pltpu.CompilerParams(vmem_limit_bytes=16 * 2**20),
    )(here, own, received, received, received)


def shards(p_blocks, p_cols):
    rows = p_blocks.shape[0]
    classes = lax.axis_size("depth")
    n_panels = lax.axis_size("row")
    matrix_rows = rows * n_panels
    r = lax.axis_index("row")
    core = lax.rem(r, 2)
    here = jnp.stack([lax.axis_index("depth"), core, (r - PANELS // 2) * rows]).astype(jnp.int32)
    blocks = p_blocks[:, 0]
    line = jnp.zeros((1, BS), jnp.bfloat16).at[0, :rows].set(p_cols[:, 0].astype(jnp.bfloat16))
    tail = jnp.broadcast_to(line, (TAIL, BS))

    own = jnp.concatenate(
        [blocks.reshape(2, rows // 2 * BS, BS), jnp.broadcast_to(tail, (2, TAIL, BS))], axis=1
    )
    down = up = own
    left = [own]
    for hop in range(3):
        down = passed_along(down, "col", 1)
        up = passed_along(up, "col", -1)
        left += [down, up]
        if hop == 0:
            after_first = (down, up)
    halves = [passed_along(down[0], "col", 1), passed_along(up[1], "col", -1)]

    pieces = blocks.reshape(rows // classes, classes, BS, BS).swapaxes(0, 1)
    pieces = jnp.concatenate(
        [pieces.reshape(classes, rows // classes * BS, BS), jnp.broadcast_to(tail, (classes, TAIL, BS))], axis=1
    )
    pieces = jnp.concatenate([pieces, pieces], axis=0)
    groups = [[(2 * z + c) * classes + x for c in range(2) for x in range(classes)] for z in range(n_panels // 2)]
    pair = lax.all_to_all(pieces, ("row", "depth"), 0, 0, axis_index_groups=groups)
    pair = pair.reshape(2 * classes * SPAN, BS)
    pair, *_ = lax.optimization_barrier((pair,) + after_first)
    far = lax.ppermute(pair, "row", [(i, (i + (2 if i % 2 == 0 else -2)) % n_panels) for i in range(n_panels)])
    panel = classes * SPAN
    cross = jnp.where(core == 0, pair[:panel], pair[panel:])
    cross = lax.ppermute(cross, "row", [(i, (i + (-2 if i % 2 == 0 else 2)) % n_panels) for i in range(n_panels)])

    coded, mine = products(here, left, halves, (pair, far, cross), rows, classes, matrix_rows)
    received = lax.all_to_all(coded, "depth", 0, 0)
    return summed(here, mine, received, rows, classes).reshape(rows, 1, BS, BS)


def solution(mesh):
    return jax.shard_map(
        shards,
        mesh=mesh,
        in_specs=(P("row", ("col", "depth"), None, None), P("row", ("col", "depth"))),
        out_specs=P("row", ("col", "depth"), None, None),
        check_vma=False,
    )
```

```python
import functools

import jax
import jax.numpy as jnp
from jax import lax
from jax.experimental import pallas as pl
from jax.experimental.pallas import tpu as pltpu
from jax.sharding import PartitionSpec as P

BS = 128
TAIL = 16
STEP = 4
PART_ROWS = 16
PANELS = 5
SPAN = 4 * BS + TAIL
QMAX = 32700.0
TINY = 2.0**-111


def passed_along(block, axis, distance):
    n = lax.axis_size(axis)
    return lax.ppermute(block, axis, [(i, (i + distance) % n) for i in range(n)])


def offsets(left_tails, window_tails, x, anchor, matrix_rows, classes, zero_at):
    sub = lax.broadcasted_iota(jnp.int32, (8, BS), 0)
    lane = lax.broadcasted_iota(jnp.int32, (8, BS), 1)

    def numbers(tile):
        return tile.astype(jnp.float32)[:8].astype(jnp.int32)

    cols = jnp.zeros((8, BS), jnp.int32)
    for s in range(8):
        cols = jnp.where(sub == s, numbers(left_tails[s]), cols)
    place = lax.shift_right_logical((cols - anchor + 2 * matrix_rows) & (matrix_rows - 1), 2)
    base = lax.shift_right_logical(place, 2) * (classes * SPAN) + (place & 3) * BS
    result = []
    for m in range(classes):
        tails = [numbers(window_tails[p * classes + m]) for p in range(PANELS)]
        found = jnp.zeros((8, BS), jnp.int32)
        for p in range(PANELS):
            for a in range(4):
                column = jnp.sum(jnp.where(lane == 4 * a + x, tails[p], 0), axis=1, keepdims=True)
                hit = (place == 4 * p + a) & (tails[PANELS // 2] == column)
                found = jnp.where(hit, 1, found)
        result.append(jnp.where(found == 1, base + m * SPAN, zero_at))
    return result


def product_kernel(first, start, half_rows, classes, matrix_rows, here_ref, *refs):
    if first:
        lefts, tail_sources, refs = refs[:9], refs[9:17], refs[17:]
        window_pieces, (pair, far, cross), refs = refs[:3], refs[3:6], refs[6:]
        q_ref, own_ref, wide, held, tails, idx_ref, sems = refs
    else:
        idx_ref, *refs = refs
        lefts, (pair, far, cross), refs = refs[:9], refs[9:12], refs[12:]
        q_ref, own_ref, held, sems = refs
    step = pl.program_id(0)
    panel = classes * SPAN
    zero_at = PANELS * panel
    x, core, anchor = here_ref[0], here_ref[1], here_ref[2]

    @pl.when(step == 0)
    def _():
        pieces = ((pair, 2 - core, 2), (far, 3 * core, 2), (cross, 4 - 4 * core, 1))
        copies, tail_copies = [], []
        if first:
            for s in range(8):
                at = pl.ds(half_rows * BS, TAIL)
                source = tail_sources[s].at[0, at] if s < 7 else tail_sources[s].at[at]
                tail_copies.append(pltpu.make_async_copy(source, tails.at[s], sems.at[s]))
            for n, (source, p, count) in enumerate(pieces):
                source = window_pieces[n].at[:, pl.ds(4 * BS, TAIL)]
                at = pl.ds(8 + p * classes, count * classes)
                tail_copies.append(pltpu.make_async_copy(source, tails.at[at], sems.at[8 + n]))
        for n, (source, p, count) in enumerate(pieces):
            at = pl.ds(pl.multiple_of(p * panel, TAIL), count * panel)
            copies.append(pltpu.make_async_copy(source, held.at[at], sems.at[11 + n]))
        for copy in tail_copies + copies:
            copy.start()
        held[pl.ds(zero_at, BS), :] = jnp.zeros((BS, BS), held.dtype)
        for copy in tail_copies:
            copy.wait()
        if first:
            left_tails = [tails[s] for s in range(8)]
            window_tails = [tails[8 + n] for n in range(PANELS * classes)]
            found = offsets(left_tails, window_tails, x, anchor, matrix_rows, classes, zero_at)
            for m in range(classes):
                wide[pl.ds(m * 8, 8), :] = found[m]
            copies.append(pltpu.make_async_copy(wide, idx_ref, sems.at[14]))
            copies[-1].start()
        for copy in copies:
            copy.wait()

    slots = [lax.rem(x + d, classes) for d in range(classes)]
    codes = [[] for _ in range(classes)]
    in_first_half = step * STEP + start < half_rows
    for r in range(STEP):
        at = slice(r * BS, (r + 1) * BS)
        row = step * STEP + r + start
        left = [ref[0, at, :] for ref in lefts[:7]]
        left.append(jnp.where(in_first_half, lefts[7][at, :], lefts[8][at, :]))
        left = jnp.concatenate(left, axis=1)
        right = []
        for d in range(classes):
            picked = []
            for s in range(8):
                k = idx_ref[slots[d] * 8 + s, row]
                picked.append(held[pl.ds(pl.multiple_of(k, TAIL), BS), :])
            right.append(jnp.concatenate(picked, axis=0))
        right = jnp.concatenate(right, axis=1)
        sums = jnp.dot(left, right, preferred_element_type=jnp.float32)
        own_ref[at, :] = sums[:, :BS]
        for d in range(1, classes):
            part = sums[:, d * BS : (d + 1) * BS]
            top = jnp.max(jnp.max(jnp.abs(part), axis=0, keepdims=True), axis=1, keepdims=True)
            code = jnp.ceil(jnp.log2(jnp.maximum(top, TINY)) * 16.0)
            scaled = part * (jnp.exp2(code * (-1.0 / 16.0)) * QMAX)
            coded = jnp.round(jnp.clip(scaled, -32767.0, 32767.0)).astype(jnp.int32)
            q_ref[slots[d], 0, at, :] = coded.astype(jnp.int16)
            codes[d].append(code)
    sub = lax.broadcasted_iota(jnp.int32, (TAIL, BS), 0)
    for d in range(1, classes):
        lines = jnp.zeros((TAIL, BS), jnp.float32)
        for r in range(STEP):
            lines = jnp.where(sub == r, codes[d][r], lines)
        q_ref[slots[d], 0, pl.ds(STEP * BS, TAIL), :] = lines.astype(jnp.int32).astype(jnp.int16)


def products(here, idx, lefts, windows, start, rows, half_rows, classes, matrix_rows):
    first = idx is None
    n_steps = rows // STEP
    per_half = half_rows // STEP
    block = STEP * BS
    anywhere = pl.BlockSpec(memory_space=pl.ANY)

    def left_at(g, *_):
        g = g + start // STEP
        return (g // per_half, g % per_half, 0)

    out_specs = [
        pl.BlockSpec((classes, 1, block + TAIL, BS), lambda g, *_: (0, g, 0, 0)),
        pl.BlockSpec((block, BS), lambda g, *_: (g, 0)),
    ]
    out_shape = [
        jax.ShapeDtypeStruct((classes, n_steps, block + TAIL, BS), jnp.int16),
        jax.ShapeDtypeStruct((rows * BS, BS), jnp.float32),
    ]
    scratch = [pltpu.VMEM((PANELS * classes * SPAN + BS, BS), jnp.bfloat16)]
    if first:
        out_specs.append(pl.BlockSpec((classes * 8, BS), lambda g, *_: (0, 0)))
        out_shape.append(jax.ShapeDtypeStruct((classes * 8, BS), jnp.int32))
        scratch += [pltpu.VMEM((8 + PANELS * classes, TAIL, BS), jnp.bfloat16), pltpu.SMEM((classes * 8, BS), jnp.int32)]
        operands = [here, *lefts, *lefts[:8], *(w.reshape(-1, SPAN, BS) for w in windows), *windows]
    else:
        operands = [here, idx, *lefts, *windows]
    grid_spec = pltpu.PrefetchScalarGridSpec(
        num_scalar_prefetch=1 if first else 2,
        grid=(n_steps,),
        in_specs=[pl.BlockSpec((1, block, BS), left_at)] * 7
        + [pl.BlockSpec((block, BS), lambda g, *_: (jnp.minimum(g + start // STEP, per_half - 1), 0))]
        + [pl.BlockSpec((block, BS), lambda g, *_: (jnp.maximum(g + start // STEP - per_half, 0), 0))]
        + [anywhere] * (14 if first else 3),
        out_specs=out_specs,
        scratch_shapes=scratch + [pltpu.SemaphoreType.DMA((15,))],
    )
    return pl.pallas_call(
        functools.partial(product_kernel, first, start, half_rows, classes, matrix_rows),
        grid_spec=grid_spec,
        out_shape=out_shape,
        compiler_params=pltpu.CompilerParams(vmem_limit_bytes=12 * 2**20),
        cost_estimate=pl.CostEstimate(
            flops=2 * rows * 32 * BS**3, bytes_accessed=12 * 2**20, transcendentals=0
        ),
    )(*operands)


def sum_kernel(n_steps, n_parts, here_ref, *refs):
    out_ref = refs[-1]

    def add(own_ref, *received):
        scales = []
        for part in received:
            code = part[0, 0, pl.ds(STEP * BS, TAIL), :].astype(jnp.int32).astype(jnp.float32)
            scales.append(jnp.exp2(code * (1.0 / 16.0)) * (1.0 / QMAX))
        for r in range(STEP):
            at = slice(r * BS, (r + 1) * BS)
            total = own_ref[at, :]
            for part, scale in zip(received, scales):
                total = total + part[0, 0, at, :].astype(jnp.int32).astype(jnp.float32) * scale[r : r + 1, :]
            out_ref[at, :] = total.astype(jnp.bfloat16)

    for n in range(n_parts):
        pl.when(pl.program_id(0) // n_steps == n)(functools.partial(add, *refs[4 * n : 4 * n + 4]))


def summed(here, parts, rows, classes):
    block = STEP * BS
    n_steps = rows // STEP
    specs, operands = [], []
    for n, (own, received) in enumerate(parts):

        def at(g, n=n):
            return jnp.clip(g - n * n_steps, 0, n_steps - 1)

        specs.append(pl.BlockSpec((block, BS), lambda g, h, at=at: (at(g), 0)))
        for d in (1, 2, 3):
            specs.append(
                pl.BlockSpec(
                    (1, 1, block + TAIL, BS), lambda g, h, at=at, d=d: (lax.rem(h[0] + d, classes), at(g), 0, 0)
                )
            )
        operands += [own, received, received, received]
    grid_spec = pltpu.PrefetchScalarGridSpec(
        num_scalar_prefetch=1,
        grid=(len(parts) * n_steps,),
        in_specs=specs,
        out_specs=pl.BlockSpec((block, BS), lambda g, h: (g, 0)),
    )
    return pl.pallas_call(
        functools.partial(sum_kernel, n_steps, len(parts)),
        grid_spec=grid_spec,
        out_shape=jax.ShapeDtypeStruct((len(parts) * rows * BS, BS), jnp.bfloat16),
        compiler_params=pltpu.CompilerParams(vmem_limit_bytes=12 * 2**20),
    )(here, *operands)


def own_payload_kernel(half_rows, cols_ref, blocks_ref, out_ref):
    shape = (cols_ref.shape[0], BS)
    own_lane = lax.broadcasted_iota(jnp.int32, shape, 0) == lax.broadcasted_iota(jnp.int32, shape, 1)
    numbers = jnp.broadcast_to(cols_ref[...], shape).astype(jnp.float32)
    line = jnp.sum(jnp.where(own_lane, numbers, 0.0), axis=0, keepdims=True)
    tail = jnp.broadcast_to(line, (TAIL, BS)).astype(jnp.bfloat16)
    span = half_rows * BS
    for half in range(2):
        out_ref[half, pl.ds(0, span), :] = blocks_ref[pl.ds(half * span, span), :]
        out_ref[half, pl.ds(span, TAIL), :] = tail


def own_payload(blocks, cols, half_rows):
    return pl.pallas_call(
        functools.partial(own_payload_kernel, half_rows),
        out_shape=jax.ShapeDtypeStruct((2, half_rows * BS + TAIL, BS), jnp.bfloat16),
        compiler_params=pltpu.CompilerParams(vmem_limit_bytes=8 * 2**20),
    )(cols, blocks)


def pieces_kernel(classes, payload_ref, out_ref):
    rows = 2 * (payload_ref.shape[1] - TAIL) // BS
    for x in range(classes):
        for n in range(rows // classes):
            row = n * classes + x
            half, at = row // (rows // 2), row % (rows // 2) * BS
            block = payload_ref[half, pl.ds(at, BS), :]
            out_ref[x, pl.ds(n * BS, BS), :] = block
            out_ref[x + classes, pl.ds(n * BS, BS), :] = block
        tail = payload_ref[0, pl.ds(rows // 2 * BS, TAIL), :]
        out_ref[x, pl.ds(4 * BS, TAIL), :] = tail
        out_ref[x + classes, pl.ds(4 * BS, TAIL), :] = tail


def residue_pieces(payload, classes):
    return pl.pallas_call(
        functools.partial(pieces_kernel, classes),
        out_shape=jax.ShapeDtypeStruct((2 * classes, SPAN, BS), jnp.bfloat16),
        compiler_params=pltpu.CompilerParams(vmem_limit_bytes=8 * 2**20),
    )(payload)


def shards(p_blocks, p_cols):
    rows = p_blocks.shape[0]
    classes = lax.axis_size("depth")
    n_panels = lax.axis_size("row")
    matrix_rows = rows * n_panels
    r = lax.axis_index("row")
    core = lax.rem(r, 2)
    here = jnp.stack([lax.axis_index("depth"), core, (r - PANELS // 2) * rows]).astype(jnp.int32)

    own = own_payload(p_blocks.reshape(rows * BS, BS), p_cols, rows // 2)
    down = up = own
    left = [own]
    for hop in range(3):
        down = passed_along(down, "col", 1)
        up = passed_along(up, "col", -1)
        left += [down, up]
        if hop == 0:
            after_first = (down, up)
    halves = [passed_along(down[0], "col", 1), passed_along(up[1], "col", -1)]

    pieces = residue_pieces(own, classes)
    groups = [[(2 * z + c) * classes + x for c in range(2) for x in range(classes)] for z in range(n_panels // 2)]
    pair = lax.all_to_all(pieces, ("row", "depth"), 0, 0, axis_index_groups=groups)
    pair = pair.reshape(2 * classes * SPAN, BS)
    pair, *_ = lax.optimization_barrier((pair,) + after_first)
    far = lax.ppermute(pair, "row", [(i, (i + (2 if i % 2 == 0 else -2)) % n_panels) for i in range(n_panels)])
    panel = classes * SPAN
    cross = jnp.where(core == 0, pair[:panel], pair[panel:])
    cross = lax.ppermute(cross, "row", [(i, (i + (-2 if i % 2 == 0 else 2)) % n_panels) for i in range(n_panels)])

    windows = (pair, far, cross)
    left[1:7] = [pltpu.with_memory_space_constraint(shard, pltpu.HBM) for shard in left[1:7]]
    idx, parts = None, []
    for start in range(0, rows, PART_ROWS):
        coded, mine, *found = products(
            here, idx, left + halves, windows, start, PART_ROWS, rows // 2, classes, matrix_rows
        )
        idx = found[0] if found else idx
        parts.append((mine, lax.all_to_all(coded, "depth", 0, 0)))
    return summed(here, parts, PART_ROWS, classes).reshape(rows, 1, BS, BS)


def solution(mesh):
    return jax.shard_map(
        shards,
        mesh=mesh,
        in_specs=(P("row", ("col", "depth"), None, None), P("row", ("col", "depth"))),
        out_specs=P("row", ("col", "depth"), None, None),
        check_vma=False,
    )
```

```python
import functools

import jax
import jax.numpy as jnp
from jax import lax
from jax.experimental import pallas as pl
from jax.experimental.pallas import tpu as pltpu
from jax.sharding import PartitionSpec as P

BS = 128
TAIL = 16
STEP = 8
PART_ROWS = 16
PANELS = 5
SPAN = 4 * BS + TAIL
QMAX = 32700.0
TINY = 2.0**-111


def passed_along(block, axis, distance):
    n = lax.axis_size(axis)
    return lax.ppermute(block, axis, [(i, (i + distance) % n) for i in range(n)])


def offsets(left_tails, window_tails, x, anchor, matrix_rows, classes, zero_at):
    sub = lax.broadcasted_iota(jnp.int32, (8, BS), 0)
    lane = lax.broadcasted_iota(jnp.int32, (8, BS), 1)

    def numbers(tile):
        return tile.astype(jnp.float32)[:8].astype(jnp.int32)

    cols = jnp.zeros((8, BS), jnp.int32)
    for s in range(8):
        cols = jnp.where(sub == s, numbers(left_tails[s]), cols)
    place = lax.shift_right_logical((cols - anchor + 2 * matrix_rows) & (matrix_rows - 1), 2)
    base = lax.shift_right_logical(place, 2) * (classes * SPAN) + (place & 3) * BS
    result = []
    for m in range(classes):
        tails = [numbers(window_tails[p * classes + m]) for p in range(PANELS)]
        found = jnp.zeros((8, BS), jnp.int32)
        for p in range(PANELS):
            for a in range(4):
                column = jnp.sum(jnp.where(lane == 4 * a + x, tails[p], 0), axis=1, keepdims=True)
                hit = (place == 4 * p + a) & (tails[PANELS // 2] == column)
                found = jnp.where(hit, 1, found)
        result.append(jnp.where(found == 1, base + m * SPAN, zero_at))
    return result


def product_kernel(first, start, half_rows, classes, matrix_rows, here_ref, *refs):
    if first:
        lefts, tail_sources, refs = refs[:9], refs[9:17], refs[17:]
        window_pieces, (pair, far, cross), refs = refs[:3], refs[3:6], refs[6:]
        q_ref, own_ref, wide, held, tails, idx_ref, sems = refs
    else:
        idx_ref, *refs = refs
        lefts, (pair, far, cross), refs = refs[:9], refs[9:12], refs[12:]
        q_ref, own_ref, held, sems = refs
    step = pl.program_id(0)
    panel = classes * SPAN
    zero_at = PANELS * panel
    x, core, anchor = here_ref[0], here_ref[1], here_ref[2]

    @pl.when(step == 0)
    def _():
        pieces = ((pair, 2 - core, 2), (far, 3 * core, 2), (cross, 4 - 4 * core, 1))
        copies, tail_copies = [], []
        if first:
            for s in range(8):
                at = pl.ds(half_rows * BS, TAIL)
                source = tail_sources[s].at[0, at] if s < 7 else tail_sources[s].at[at]
                tail_copies.append(pltpu.make_async_copy(source, tails.at[s], sems.at[s]))
            for n, (source, p, count) in enumerate(pieces):
                source = window_pieces[n].at[:, pl.ds(4 * BS, TAIL)]
                at = pl.ds(8 + p * classes, count * classes)
                tail_copies.append(pltpu.make_async_copy(source, tails.at[at], sems.at[8 + n]))
        for n, (source, p, count) in enumerate(pieces):
            at = pl.ds(pl.multiple_of(p * panel, TAIL), count * panel)
            copies.append(pltpu.make_async_copy(source, held.at[at], sems.at[11 + n]))
        for copy in tail_copies + copies:
            copy.start()
        held[pl.ds(zero_at, BS), :] = jnp.zeros((BS, BS), held.dtype)
        for copy in tail_copies:
            copy.wait()
        if first:
            left_tails = [tails[s] for s in range(8)]
            window_tails = [tails[8 + n] for n in range(PANELS * classes)]
            found = offsets(left_tails, window_tails, x, anchor, matrix_rows, classes, zero_at)
            for m in range(classes):
                wide[pl.ds(m * 8, 8), :] = found[m]
            copies.append(pltpu.make_async_copy(wide, idx_ref, sems.at[14]))
            copies[-1].start()
        for copy in copies:
            copy.wait()

    slots = [lax.rem(x + d, classes) for d in range(classes)]
    codes = [[] for _ in range(classes)]
    in_first_half = step * STEP + start < half_rows
    for r in range(STEP):
        at = slice(r * BS, (r + 1) * BS)
        row = step * STEP + r + start
        left = [ref[0, at, :] for ref in lefts[:7]]
        left.append(jnp.where(in_first_half, lefts[7][at, :], lefts[8][at, :]))
        left = jnp.concatenate(left, axis=1)
        right = []
        for d in range(classes):
            picked = []
            for s in range(8):
                k = idx_ref[slots[d] * 8 + s, row]
                picked.append(held[pl.ds(pl.multiple_of(k, TAIL), BS), :])
            right.append(jnp.concatenate(picked, axis=0))
        right = jnp.concatenate(right, axis=1)
        sums = jnp.dot(left, right, preferred_element_type=jnp.float32)
        own_ref[at, :] = sums[:, :BS]
        for d in range(1, classes):
            part = sums[:, d * BS : (d + 1) * BS]
            top = jnp.max(jnp.max(jnp.abs(part), axis=0, keepdims=True), axis=1, keepdims=True)
            code = jnp.ceil(jnp.log2(jnp.maximum(top, TINY)) * 16.0)
            scaled = part * (jnp.exp2(code * (-1.0 / 16.0)) * QMAX)
            coded = jnp.round(scaled).astype(jnp.int32)
            q_ref[slots[d], 0, at, :] = coded.astype(jnp.int16)
            codes[d].append(code)
    sub = lax.broadcasted_iota(jnp.int32, (TAIL, BS), 0)
    for d in range(1, classes):
        lines = jnp.zeros((TAIL, BS), jnp.float32)
        for r in range(STEP):
            lines = jnp.where(sub == r, codes[d][r], lines)
        q_ref[slots[d], 0, pl.ds(STEP * BS, TAIL), :] = lines.astype(jnp.int32).astype(jnp.int16)


def products(here, idx, lefts, windows, start, rows, half_rows, classes, matrix_rows):
    first = idx is None
    n_steps = rows // STEP
    per_half = half_rows // STEP
    block = STEP * BS
    anywhere = pl.BlockSpec(memory_space=pl.ANY)

    def left_at(g, *_):
        g = g + start // STEP
        return (g // per_half, g % per_half, 0)

    out_specs = [
        pl.BlockSpec((classes, 1, block + TAIL, BS), lambda g, *_: (0, g, 0, 0)),
        pl.BlockSpec((block, BS), lambda g, *_: (g, 0)),
    ]
    out_shape = [
        jax.ShapeDtypeStruct((classes, n_steps, block + TAIL, BS), jnp.int16),
        jax.ShapeDtypeStruct((rows * BS, BS), jnp.float32),
    ]
    scratch = [pltpu.VMEM((PANELS * classes * SPAN + BS, BS), jnp.bfloat16)]
    if first:
        out_specs.append(pl.BlockSpec((classes * 8, BS), lambda g, *_: (0, 0)))
        out_shape.append(jax.ShapeDtypeStruct((classes * 8, BS), jnp.int32))
        scratch += [pltpu.VMEM((8 + PANELS * classes, TAIL, BS), jnp.bfloat16), pltpu.SMEM((classes * 8, BS), jnp.int32)]
        operands = [here, *lefts, *lefts[:8], *(w.reshape(-1, SPAN, BS) for w in windows), *windows]
    else:
        operands = [here, idx, *lefts, *windows]
    grid_spec = pltpu.PrefetchScalarGridSpec(
        num_scalar_prefetch=1 if first else 2,
        grid=(n_steps,),
        in_specs=[pl.BlockSpec((1, block, BS), left_at)] * 7
        + [pl.BlockSpec((block, BS), lambda g, *_: (jnp.minimum(g + start // STEP, per_half - 1), 0))]
        + [pl.BlockSpec((block, BS), lambda g, *_: (jnp.maximum(g + start // STEP - per_half, 0), 0))]
        + [anywhere] * (14 if first else 3),
        out_specs=out_specs,
        scratch_shapes=scratch + [pltpu.SemaphoreType.DMA((15,))],
    )
    return pl.pallas_call(
        functools.partial(product_kernel, first, start, half_rows, classes, matrix_rows),
        grid_spec=grid_spec,
        out_shape=out_shape,
        compiler_params=pltpu.CompilerParams(vmem_limit_bytes=20 * 2**20),
        cost_estimate=pl.CostEstimate(
            flops=2 * rows * 32 * BS**3, bytes_accessed=12 * 2**20, transcendentals=0
        ),
    )(*operands)


def sum_kernel(n_steps, n_parts, here_ref, *refs):
    out_ref = refs[-1]

    def add(own_ref, *received):
        scales = []
        for part in received:
            code = part[0, 0, pl.ds(STEP * BS, TAIL), :].astype(jnp.int32).astype(jnp.float32)
            scales.append(jnp.exp2(code * (1.0 / 16.0)) * (1.0 / QMAX))
        for r in range(STEP):
            at = slice(r * BS, (r + 1) * BS)
            total = own_ref[at, :]
            for part, scale in zip(received, scales):
                total = total + part[0, 0, at, :].astype(jnp.int32).astype(jnp.float32) * scale[r : r + 1, :]
            out_ref[at, :] = total.astype(jnp.bfloat16)

    for n in range(n_parts):
        pl.when(pl.program_id(0) // n_steps == n)(functools.partial(add, *refs[4 * n : 4 * n + 4]))


def summed(here, parts, rows, classes):
    block = STEP * BS
    n_steps = rows // STEP
    specs, operands = [], []
    for n, (own, received) in enumerate(parts):

        def at(g, n=n):
            return jnp.clip(g - n * n_steps, 0, n_steps - 1)

        specs.append(pl.BlockSpec((block, BS), lambda g, h, at=at: (at(g), 0)))
        for d in (1, 2, 3):
            specs.append(
                pl.BlockSpec(
                    (1, 1, block + TAIL, BS), lambda g, h, at=at, d=d: (lax.rem(h[0] + d, classes), at(g), 0, 0)
                )
            )
        operands += [own, received, received, received]
    grid_spec = pltpu.PrefetchScalarGridSpec(
        num_scalar_prefetch=1,
        grid=(len(parts) * n_steps,),
        in_specs=specs,
        out_specs=pl.BlockSpec((block, BS), lambda g, h: (g, 0)),
    )
    return pl.pallas_call(
        functools.partial(sum_kernel, n_steps, len(parts)),
        grid_spec=grid_spec,
        out_shape=jax.ShapeDtypeStruct((len(parts) * rows * BS, BS), jnp.bfloat16),
        compiler_params=pltpu.CompilerParams(vmem_limit_bytes=12 * 2**20),
    )(here, *operands)


def own_payload_kernel(half_rows, cols_ref, blocks_ref, out_ref):
    shape = (cols_ref.shape[0], BS)
    own_lane = lax.broadcasted_iota(jnp.int32, shape, 0) == lax.broadcasted_iota(jnp.int32, shape, 1)
    numbers = jnp.broadcast_to(cols_ref[...], shape).astype(jnp.float32)
    line = jnp.sum(jnp.where(own_lane, numbers, 0.0), axis=0, keepdims=True)
    tail = jnp.broadcast_to(line, (TAIL, BS)).astype(jnp.bfloat16)
    span = half_rows * BS
    for half in range(2):
        out_ref[half, pl.ds(0, span), :] = blocks_ref[pl.ds(half * span, span), :]
        out_ref[half, pl.ds(span, TAIL), :] = tail


def own_payload(blocks, cols, half_rows):
    return pl.pallas_call(
        functools.partial(own_payload_kernel, half_rows),
        out_shape=jax.ShapeDtypeStruct((2, half_rows * BS + TAIL, BS), jnp.bfloat16),
        compiler_params=pltpu.CompilerParams(vmem_limit_bytes=8 * 2**20),
    )(cols, blocks)


def pieces_kernel(classes, payload_ref, out_ref):
    rows = 2 * (payload_ref.shape[1] - TAIL) // BS
    for x in range(classes):
        for n in range(rows // classes):
            row = n * classes + x
            half, at = row // (rows // 2), row % (rows // 2) * BS
            block = payload_ref[half, pl.ds(at, BS), :]
            out_ref[x, pl.ds(n * BS, BS), :] = block
            out_ref[x + classes, pl.ds(n * BS, BS), :] = block
        tail = payload_ref[0, pl.ds(rows // 2 * BS, TAIL), :]
        out_ref[x, pl.ds(4 * BS, TAIL), :] = tail
        out_ref[x + classes, pl.ds(4 * BS, TAIL), :] = tail


def residue_pieces(payload, classes):
    return pl.pallas_call(
        functools.partial(pieces_kernel, classes),
        out_shape=jax.ShapeDtypeStruct((2 * classes, SPAN, BS), jnp.bfloat16),
        compiler_params=pltpu.CompilerParams(vmem_limit_bytes=8 * 2**20),
    )(payload)


def shards(p_blocks, p_cols):
    rows = p_blocks.shape[0]
    classes = lax.axis_size("depth")
    n_panels = lax.axis_size("row")
    matrix_rows = rows * n_panels
    r = lax.axis_index("row")
    core = lax.rem(r, 2)
    here = jnp.stack([lax.axis_index("depth"), core, (r - PANELS // 2) * rows]).astype(jnp.int32)

    own = own_payload(p_blocks.reshape(rows * BS, BS), p_cols, rows // 2)
    down = up = own
    left = [own]
    for hop in range(3):
        down = passed_along(down, "col", 1)
        up = passed_along(up, "col", -1)
        left += [down, up]
        if hop == 0:
            after_first = (down, up)
    halves = [passed_along(down[0], "col", 1), passed_along(up[1], "col", -1)]

    pieces = residue_pieces(own, classes)
    groups = [[(2 * z + c) * classes + x for c in range(2) for x in range(classes)] for z in range(n_panels // 2)]
    pair = lax.all_to_all(pieces, ("row", "depth"), 0, 0, axis_index_groups=groups)
    pair = pair.reshape(2 * classes * SPAN, BS)
    pair, *_ = lax.optimization_barrier((pair,) + after_first)
    far = lax.ppermute(pair, "row", [(i, (i + (2 if i % 2 == 0 else -2)) % n_panels) for i in range(n_panels)])
    panel = classes * SPAN
    cross = jnp.where(core == 0, pair[:panel], pair[panel:])
    cross = lax.ppermute(cross, "row", [(i, (i + (-2 if i % 2 == 0 else 2)) % n_panels) for i in range(n_panels)])

    windows = (pair, far, cross)
    left[1:7] = [pltpu.with_memory_space_constraint(shard, pltpu.HBM) for shard in left[1:7]]
    idx, parts = None, []
    for start in range(0, rows, PART_ROWS):
        coded, mine, *found = products(
            here, idx, left + halves, windows, start, PART_ROWS, rows // 2, classes, matrix_rows
        )
        idx = found[0] if found else idx
        parts.append((mine, lax.all_to_all(coded, "depth", 0, 0)))
    return summed(here, parts, PART_ROWS, classes).reshape(rows, 1, BS, BS)


def solution(mesh):
    return jax.shard_map(
        shards,
        mesh=mesh,
        in_specs=(P("row", ("col", "depth"), None, None), P("row", ("col", "depth"))),
        out_specs=P("row", ("col", "depth"), None, None),
        check_vma=False,
    )
```

```python
import functools

import jax
import jax.numpy as jnp
from jax import lax
from jax.experimental import pallas as pl
from jax.experimental.pallas import tpu as pltpu
from jax.sharding import PartitionSpec as P

BS = 128
TAIL = 16
STEP = 8
PART_ROWS = 16
PANELS = 5
SPAN = 4 * BS + TAIL
QMAX = 32700.0
TINY = 2.0**-111


def passed_along(block, axis, distance):
    n = lax.axis_size(axis)
    return lax.ppermute(block, axis, [(i, (i + distance) % n) for i in range(n)])


def offsets(left_tails, window_tails, x, anchor, matrix_rows, classes, zero_at):
    sub = lax.broadcasted_iota(jnp.int32, (8, BS), 0)
    lane = lax.broadcasted_iota(jnp.int32, (8, BS), 1)

    def numbers(tile):
        return tile.astype(jnp.float32)[:8].astype(jnp.int32)

    cols = jnp.zeros((8, BS), jnp.int32)
    for s in range(8):
        cols = jnp.where(sub == s, numbers(left_tails[s]), cols)
    place = lax.shift_right_logical((cols - anchor + 2 * matrix_rows) & (matrix_rows - 1), 2)
    base = lax.shift_right_logical(place, 2) * (classes * SPAN) + (place & 3) * BS
    result = []
    for m in range(classes):
        tails = [numbers(window_tails[p * classes + m]) for p in range(PANELS)]
        found = jnp.zeros((8, BS), jnp.int32)
        for p in range(PANELS):
            for a in range(4):
                column = jnp.sum(jnp.where(lane == 4 * a + x, tails[p], 0), axis=1, keepdims=True)
                hit = (place == 4 * p + a) & (tails[PANELS // 2] == column)
                found = jnp.where(hit, 1, found)
        result.append(jnp.where(found == 1, base + m * SPAN, zero_at))
    return result


def product_kernel(first, start, half_rows, classes, matrix_rows, here_ref, *refs):
    if first:
        lefts, tail_sources, refs = refs[:9], refs[9:17], refs[17:]
        window_pieces, (pair, far, cross), refs = refs[:3], refs[3:6], refs[6:]
        q_ref, own_ref, wide, held, tails, idx_ref, sems = refs
    else:
        idx_ref, *refs = refs
        lefts, (pair, far, cross), refs = refs[:9], refs[9:12], refs[12:]
        q_ref, own_ref, held, sems = refs
    step = pl.program_id(0)
    panel = classes * SPAN
    zero_at = PANELS * panel
    x, core, anchor = here_ref[0], here_ref[1], here_ref[2]

    @pl.when(step == 0)
    def _():
        pieces = ((pair, 2 - core, 2), (far, 3 * core, 2), (cross, 4 - 4 * core, 1))
        copies, tail_copies = [], []
        if first:
            for s in range(8):
                at = pl.ds(half_rows * BS, TAIL)
                source = tail_sources[s].at[0, at] if s < 7 else tail_sources[s].at[at]
                tail_copies.append(pltpu.make_async_copy(source, tails.at[s], sems.at[s]))
            for n, (source, p, count) in enumerate(pieces):
                source = window_pieces[n].at[:, pl.ds(4 * BS, TAIL)]
                at = pl.ds(8 + p * classes, count * classes)
                tail_copies.append(pltpu.make_async_copy(source, tails.at[at], sems.at[8 + n]))
        for n, (source, p, count) in enumerate(pieces):
            at = pl.ds(pl.multiple_of(p * panel, TAIL), count * panel)
            copies.append(pltpu.make_async_copy(source, held.at[at], sems.at[11 + n]))
        for copy in tail_copies + copies:
            copy.start()
        held[pl.ds(zero_at, BS), :] = jnp.zeros((BS, BS), held.dtype)
        for copy in tail_copies:
            copy.wait()
        if first:
            left_tails = [tails[s] for s in range(8)]
            window_tails = [tails[8 + n] for n in range(PANELS * classes)]
            found = offsets(left_tails, window_tails, x, anchor, matrix_rows, classes, zero_at)
            for m in range(classes):
                wide[pl.ds(m * 8, 8), :] = found[m]
            copies.append(pltpu.make_async_copy(wide, idx_ref, sems.at[14]))
            copies[-1].start()
        for copy in copies:
            copy.wait()

    slots = [lax.rem(x + d, classes) for d in range(classes)]
    codes = [[] for _ in range(classes)]
    in_first_half = step * STEP + start < half_rows
    for r in range(STEP):
        at = slice(r * BS, (r + 1) * BS)
        row = step * STEP + r + start
        left = [ref[0, at, :] for ref in lefts[:7]]
        left.append(jnp.where(in_first_half, lefts[7][at, :], lefts[8][at, :]))
        left = jnp.concatenate(left, axis=1)
        right = []
        for d in range(classes):
            picked = []
            for s in range(8):
                k = idx_ref[slots[d] * 8 + s, row]
                picked.append(held[pl.ds(pl.multiple_of(k, TAIL), BS), :])
            right.append(jnp.concatenate(picked, axis=0))
        right = jnp.concatenate(right, axis=1)
        sums = jnp.dot(left, right, preferred_element_type=jnp.float32)
        own_ref[at, :] = sums[:, :BS]
        for d in range(1, classes):
            part = sums[:, d * BS : (d + 1) * BS]
            top = jnp.max(jnp.max(jnp.abs(part), axis=0, keepdims=True), axis=1, keepdims=True)
            code = jnp.ceil(jnp.log2(jnp.maximum(top, TINY)) * 16.0)
            scaled = part * (jnp.exp2(code * (-1.0 / 16.0)) * QMAX)
            coded = jnp.round(scaled).astype(jnp.int32)
            q_ref[slots[d], 0, at, :] = coded.astype(jnp.int16)
            codes[d].append(code)
    sub = lax.broadcasted_iota(jnp.int32, (TAIL, BS), 0)
    for d in range(1, classes):
        lines = jnp.zeros((TAIL, BS), jnp.float32)
        for r in range(STEP):
            lines = jnp.where(sub == r, codes[d][r], lines)
        q_ref[slots[d], 0, pl.ds(STEP * BS, TAIL), :] = lines.astype(jnp.int32).astype(jnp.int16)


def products(here, idx, lefts, windows, start, rows, half_rows, classes, matrix_rows):
    first = idx is None
    n_steps = rows // STEP
    per_half = half_rows // STEP
    block = STEP * BS
    anywhere = pl.BlockSpec(memory_space=pl.ANY)

    def left_at(g, *_):
        g = g + start // STEP
        return (g // per_half, g % per_half, 0)

    out_specs = [
        pl.BlockSpec((classes, 1, block + TAIL, BS), lambda g, *_: (0, g, 0, 0)),
        pl.BlockSpec((block, BS), lambda g, *_: (g, 0)),
    ]
    out_shape = [
        jax.ShapeDtypeStruct((classes, n_steps, block + TAIL, BS), jnp.int16),
        jax.ShapeDtypeStruct((rows * BS, BS), jnp.float32),
    ]
    scratch = [pltpu.VMEM((PANELS * classes * SPAN + BS, BS), jnp.bfloat16)]
    if first:
        out_specs.append(pl.BlockSpec((classes * 8, BS), lambda g, *_: (0, 0)))
        out_shape.append(jax.ShapeDtypeStruct((classes * 8, BS), jnp.int32))
        scratch += [pltpu.VMEM((8 + PANELS * classes, TAIL, BS), jnp.bfloat16), pltpu.SMEM((classes * 8, BS), jnp.int32)]
        operands = [here, *lefts, *lefts[:8], *(w.reshape(-1, SPAN, BS) for w in windows), *windows]
    else:
        operands = [here, idx, *lefts, *windows]
    grid_spec = pltpu.PrefetchScalarGridSpec(
        num_scalar_prefetch=1 if first else 2,
        grid=(n_steps,),
        in_specs=[pl.BlockSpec((1, block, BS), left_at)] * 7
        + [pl.BlockSpec((block, BS), lambda g, *_: (jnp.minimum(g + start // STEP, per_half - 1), 0))]
        + [pl.BlockSpec((block, BS), lambda g, *_: (jnp.maximum(g + start // STEP - per_half, 0), 0))]
        + [anywhere] * (14 if first else 3),
        out_specs=out_specs,
        scratch_shapes=scratch + [pltpu.SemaphoreType.DMA((15,))],
    )
    return pl.pallas_call(
        functools.partial(product_kernel, first, start, half_rows, classes, matrix_rows),
        grid_spec=grid_spec,
        out_shape=out_shape,
        compiler_params=pltpu.CompilerParams(vmem_limit_bytes=20 * 2**20),
        cost_estimate=pl.CostEstimate(
            flops=2 * rows * 32 * BS**3, bytes_accessed=12 * 2**20, transcendentals=0
        ),
    )(*operands)


def sum_kernel(n_steps, n_parts, here_ref, *refs):
    out_ref = refs[-1]

    def add(own_ref, *received):
        scales = []
        for part in received:
            code = part[0, 0, pl.ds(STEP * BS, TAIL), :].astype(jnp.int32).astype(jnp.float32)
            scales.append(jnp.exp2(code * (1.0 / 16.0)) * (1.0 / QMAX))
        for r in range(STEP):
            at = slice(r * BS, (r + 1) * BS)
            total = own_ref[at, :]
            for part, scale in zip(received, scales):
                total = total + part[0, 0, at, :].astype(jnp.int32).astype(jnp.float32) * scale[r : r + 1, :]
            out_ref[at, :] = total.astype(jnp.bfloat16)

    for n in range(n_parts):
        pl.when(pl.program_id(0) // n_steps == n)(functools.partial(add, *refs[4 * n : 4 * n + 4]))


def summed(here, parts, rows, classes):
    block = STEP * BS
    n_steps = rows // STEP
    specs, operands = [], []
    for n, (own, received) in enumerate(parts):

        def at(g, n=n):
            return jnp.clip(g - n * n_steps, 0, n_steps - 1)

        specs.append(pl.BlockSpec((block, BS), lambda g, h, at=at: (at(g), 0)))
        for d in (1, 2, 3):
            specs.append(
                pl.BlockSpec(
                    (1, 1, block + TAIL, BS), lambda g, h, at=at, d=d: (lax.rem(h[0] + d, classes), at(g), 0, 0)
                )
            )
        operands += [own, received, received, received]
    grid_spec = pltpu.PrefetchScalarGridSpec(
        num_scalar_prefetch=1,
        grid=(len(parts) * n_steps,),
        in_specs=specs,
        out_specs=pl.BlockSpec((block, BS), lambda g, h: (g, 0)),
    )
    return pl.pallas_call(
        functools.partial(sum_kernel, n_steps, len(parts)),
        grid_spec=grid_spec,
        out_shape=jax.ShapeDtypeStruct((len(parts) * rows * BS, BS), jnp.bfloat16),
        compiler_params=pltpu.CompilerParams(vmem_limit_bytes=12 * 2**20),
    )(here, *operands)


def own_payload_kernel(half_rows, cols_ref, blocks_ref, out_ref, sems):
    span = half_rows * BS
    copies = []
    for half in range(2):
        source, target = blocks_ref.at[pl.ds(half * span, span)], out_ref.at[half, pl.ds(0, span)]
        copies.append(pltpu.make_async_copy(source, target, sems.at[half]))
        copies[-1].start()
    rows = cols_ref.shape[1]
    numbers = jnp.broadcast_to(cols_ref[...].astype(jnp.float32), (TAIL, rows)).astype(jnp.bfloat16)
    for half in range(2):
        out_ref[half, pl.ds(span, TAIL), :] = jnp.zeros((TAIL, BS), jnp.bfloat16)
        out_ref[half, pl.ds(span, TAIL), pl.ds(0, rows)] = numbers
    for copy in copies:
        copy.wait()


def own_payload(blocks, cols, half_rows):
    return pl.pallas_call(
        functools.partial(own_payload_kernel, half_rows),
        in_specs=[pl.BlockSpec(memory_space=pltpu.VMEM), pl.BlockSpec(memory_space=pl.ANY)],
        out_shape=jax.ShapeDtypeStruct((2, half_rows * BS + TAIL, BS), jnp.bfloat16),
        scratch_shapes=[pltpu.SemaphoreType.DMA((2,))],
        compiler_params=pltpu.CompilerParams(vmem_limit_bytes=8 * 2**20),
    )(cols, blocks)


def pieces_kernel(classes, payload_ref, out_ref):
    rows = 2 * (payload_ref.shape[1] - TAIL) // BS
    for x in range(classes):
        for n in range(rows // classes):
            row = n * classes + x
            half, at = row // (rows // 2), row % (rows // 2) * BS
            block = payload_ref[half, pl.ds(at, BS), :]
            out_ref[x, pl.ds(n * BS, BS), :] = block
            out_ref[x + classes, pl.ds(n * BS, BS), :] = block
        tail = payload_ref[0, pl.ds(rows // 2 * BS, TAIL), :]
        out_ref[x, pl.ds(4 * BS, TAIL), :] = tail
        out_ref[x + classes, pl.ds(4 * BS, TAIL), :] = tail


def residue_pieces(payload, classes):
    return pl.pallas_call(
        functools.partial(pieces_kernel, classes),
        out_shape=jax.ShapeDtypeStruct((2 * classes, SPAN, BS), jnp.bfloat16),
        compiler_params=pltpu.CompilerParams(vmem_limit_bytes=8 * 2**20),
    )(payload)


def shards(p_blocks, p_cols):
    rows = p_blocks.shape[0]
    classes = lax.axis_size("depth")
    n_panels = lax.axis_size("row")
    matrix_rows = rows * n_panels
    r = lax.axis_index("row")
    core = lax.rem(r, 2)
    here = jnp.stack([lax.axis_index("depth"), core, (r - PANELS // 2) * rows]).astype(jnp.int32)

    blocks = pltpu.with_memory_space_constraint(p_blocks.reshape(rows * BS, BS), pltpu.HBM)
    own = own_payload(blocks, p_cols.reshape(1, rows), rows // 2)
    down = up = own
    left = [own]
    for hop in range(3):
        down = passed_along(down, "col", 1)
        up = passed_along(up, "col", -1)
        left += [down, up]
        if hop == 0:
            after_first = (down, up)
    halves = [passed_along(down[0], "col", 1), passed_along(up[1], "col", -1)]

    pieces = residue_pieces(own, classes)
    groups = [[(2 * z + c) * classes + x for c in range(2) for x in range(classes)] for z in range(n_panels // 2)]
    pair = lax.all_to_all(pieces, ("row", "depth"), 0, 0, axis_index_groups=groups)
    pair = pair.reshape(2 * classes * SPAN, BS)
    pair, *_ = lax.optimization_barrier((pair,) + after_first)
    far = lax.ppermute(pair, "row", [(i, (i + (2 if i % 2 == 0 else -2)) % n_panels) for i in range(n_panels)])
    panel = classes * SPAN
    cross = jnp.where(core == 0, pair[:panel], pair[panel:])
    cross = lax.ppermute(cross, "row", [(i, (i + (-2 if i % 2 == 0 else 2)) % n_panels) for i in range(n_panels)])

    windows = (pair, far, cross)
    left[1:7] = [pltpu.with_memory_space_constraint(shard, pltpu.HBM) for shard in left[1:7]]
    idx, parts = None, []
    for start in range(0, rows, PART_ROWS):
        coded, mine, *found = products(
            here, idx, left + halves, windows, start, PART_ROWS, rows // 2, classes, matrix_rows
        )
        idx = found[0] if found else idx
        parts.append((mine, lax.all_to_all(coded, "depth", 0, 0)))
    return summed(here, parts, PART_ROWS, classes).reshape(rows, 1, BS, BS)


def solution(mesh):
    return jax.shard_map(
        shards,
        mesh=mesh,
        in_specs=(P("row", ("col", "depth"), None, None), P("row", ("col", "depth"))),
        out_specs=P("row", ("col", "depth"), None, None),
        check_vma=False,
    )
```

```python
import functools

import jax
import jax.numpy as jnp
from jax import lax
from jax.experimental import pallas as pl
from jax.experimental.pallas import tpu as pltpu
from jax.sharding import PartitionSpec as P

BS = 128
TAIL = 16
STEP = 8
PART_ROWS = 16
PANELS = 5
SPAN = 4 * BS + TAIL
QMAX = 32700.0
TINY = 2.0**-111


def passed_along(block, axis, distance):
    n = lax.axis_size(axis)
    return lax.ppermute(block, axis, [(i, (i + distance) % n) for i in range(n)])


def offsets(left_tails, window_tails, x, anchor, matrix_rows, classes, zero_at):
    sub = lax.broadcasted_iota(jnp.int32, (8, BS), 0)
    lane = lax.broadcasted_iota(jnp.int32, (8, BS), 1)

    def numbers(tile):
        return tile.astype(jnp.float32)[:8].astype(jnp.int32)

    cols = jnp.zeros((8, BS), jnp.int32)
    for s in range(8):
        cols = jnp.where(sub == s, numbers(left_tails[s]), cols)
    place = lax.shift_right_logical((cols - anchor + 2 * matrix_rows) & (matrix_rows - 1), 2)
    base = lax.shift_right_logical(place, 2) * (classes * SPAN) + (place & 3) * BS
    result = []
    for m in range(classes):
        tails = [numbers(window_tails[p * classes + m]) for p in range(PANELS)]
        found = jnp.zeros((8, BS), jnp.int32)
        for p in range(PANELS):
            for a in range(4):
                column = jnp.sum(jnp.where(lane == 4 * a + x, tails[p], 0), axis=1, keepdims=True)
                hit = (place == 4 * p + a) & (tails[PANELS // 2] == column)
                found = jnp.where(hit, 1, found)
        result.append(jnp.where(found == 1, base + m * SPAN, zero_at))
    return result


def product_kernel(first, start, half_rows, classes, matrix_rows, here_ref, *refs):
    if first:
        lefts, tail_sources, refs = refs[:9], refs[9:17], refs[17:]
        window_pieces, (pair, far, cross), refs = refs[:3], refs[3:6], refs[6:]
        q_ref, own_ref, wide, held, tails, idx_ref, sems = refs
    else:
        idx_ref, *refs = refs
        lefts, (pair, far, cross), refs = refs[:9], refs[9:12], refs[12:]
        q_ref, own_ref, held, sems = refs
    step = pl.program_id(0)
    panel = classes * SPAN
    zero_at = PANELS * panel
    x, core, anchor = here_ref[0], here_ref[1], here_ref[2]

    @pl.when(step == 0)
    def _():
        pieces = ((pair, 2 - core, 2), (far, 3 * core, 2), (cross, 4 - 4 * core, 1))
        copies, tail_copies = [], []
        if first:
            for s in range(8):
                at = pl.ds(half_rows * BS, TAIL)
                source = tail_sources[s].at[0, at] if s < 7 else tail_sources[s].at[at]
                tail_copies.append(pltpu.make_async_copy(source, tails.at[s], sems.at[s]))
            for n, (source, p, count) in enumerate(pieces):
                source = window_pieces[n].at[:, pl.ds(4 * BS, TAIL)]
                at = pl.ds(8 + p * classes, count * classes)
                tail_copies.append(pltpu.make_async_copy(source, tails.at[at], sems.at[8 + n]))
        for n, (source, p, count) in enumerate(pieces):
            at = pl.ds(pl.multiple_of(p * panel, TAIL), count * panel)
            copies.append(pltpu.make_async_copy(source, held.at[at], sems.at[11 + n]))
        for copy in tail_copies + copies:
            copy.start()
        held[pl.ds(zero_at, BS), :] = jnp.zeros((BS, BS), held.dtype)
        for copy in tail_copies:
            copy.wait()
        if first:
            left_tails = [tails[s] for s in range(8)]
            window_tails = [tails[8 + n] for n in range(PANELS * classes)]
            found = offsets(left_tails, window_tails, x, anchor, matrix_rows, classes, zero_at)
            for m in range(classes):
                wide[pl.ds(m * 8, 8), :] = found[m]
            copies.append(pltpu.make_async_copy(wide, idx_ref, sems.at[14]))
            copies[-1].start()
        for copy in copies:
            copy.wait()

    slots = [lax.rem(x + d, classes) for d in range(classes)]
    codes = [[] for _ in range(classes)]
    in_first_half = step * STEP + start < half_rows
    for r in range(STEP):
        at = slice(r * BS, (r + 1) * BS)
        row = step * STEP + r + start
        left = [ref[0, at, :] for ref in lefts[:7]]
        left.append(jnp.where(in_first_half, lefts[7][at, :], lefts[8][at, :]))
        left = jnp.concatenate(left, axis=1)
        right = []
        for d in range(classes):
            picked = []
            for s in range(8):
                k = idx_ref[slots[d] * 8 + s, row]
                picked.append(held[pl.ds(pl.multiple_of(k, TAIL), BS), :])
            right.append(jnp.concatenate(picked, axis=0))
        right = jnp.concatenate(right, axis=1)
        sums = jnp.dot(left, right, preferred_element_type=jnp.float32)
        own_ref[at, :] = sums[:, :BS]
        for d in range(1, classes):
            part = sums[:, d * BS : (d + 1) * BS]
            top = jnp.max(jnp.max(jnp.abs(part), axis=0, keepdims=True), axis=1, keepdims=True)
            code = jnp.ceil(jnp.log2(jnp.maximum(top, TINY)) * 16.0)
            scaled = part * (jnp.exp2(code * (-1.0 / 16.0)) * QMAX)
            coded = jnp.round(scaled).astype(jnp.int32)
            q_ref[slots[d], 0, at, :] = coded.astype(jnp.int16)
            codes[d].append(code)
    sub = lax.broadcasted_iota(jnp.int32, (TAIL, BS), 0)
    for d in range(1, classes):
        lines = jnp.zeros((TAIL, BS), jnp.float32)
        for r in range(STEP):
            lines = jnp.where(sub == r, codes[d][r], lines)
        q_ref[slots[d], 0, pl.ds(STEP * BS, TAIL), :] = lines.astype(jnp.int32).astype(jnp.int16)


def products(here, idx, lefts, windows, start, rows, half_rows, classes, matrix_rows):
    first = idx is None
    n_steps = rows // STEP
    per_half = half_rows // STEP
    block = STEP * BS
    anywhere = pl.BlockSpec(memory_space=pl.ANY)

    def left_at(g, *_):
        g = g + start // STEP
        return (g // per_half, g % per_half, 0)

    out_specs = [
        pl.BlockSpec((classes, 1, block + TAIL, BS), lambda g, *_: (0, g, 0, 0)),
        pl.BlockSpec((block, BS), lambda g, *_: (g, 0)),
    ]
    out_shape = [
        jax.ShapeDtypeStruct((classes, n_steps, block + TAIL, BS), jnp.int16),
        jax.ShapeDtypeStruct((rows * BS, BS), jnp.float32),
    ]
    scratch = [pltpu.VMEM((PANELS * classes * SPAN + BS, BS), jnp.bfloat16)]
    if first:
        out_specs.append(pl.BlockSpec((classes * 8, BS), lambda g, *_: (0, 0)))
        out_shape.append(jax.ShapeDtypeStruct((classes * 8, BS), jnp.int32))
        scratch += [pltpu.VMEM((8 + PANELS * classes, TAIL, BS), jnp.bfloat16), pltpu.SMEM((classes * 8, BS), jnp.int32)]
        operands = [here, *lefts, *lefts[:8], *(w.reshape(-1, SPAN, BS) for w in windows), *windows]
    else:
        operands = [here, idx, *lefts, *windows]
    grid_spec = pltpu.PrefetchScalarGridSpec(
        num_scalar_prefetch=1 if first else 2,
        grid=(n_steps,),
        in_specs=[pl.BlockSpec((1, block, BS), left_at)] * 7
        + [pl.BlockSpec((block, BS), lambda g, *_: (jnp.minimum(g + start // STEP, per_half - 1), 0))]
        + [pl.BlockSpec((block, BS), lambda g, *_: (jnp.maximum(g + start // STEP - per_half, 0), 0))]
        + [anywhere] * (14 if first else 3),
        out_specs=out_specs,
        scratch_shapes=scratch + [pltpu.SemaphoreType.DMA((15,))],
    )
    return pl.pallas_call(
        functools.partial(product_kernel, first, start, half_rows, classes, matrix_rows),
        grid_spec=grid_spec,
        out_shape=out_shape,
        compiler_params=pltpu.CompilerParams(vmem_limit_bytes=20 * 2**20),
        cost_estimate=pl.CostEstimate(
            flops=2 * rows * 32 * BS**3, bytes_accessed=12 * 2**20, transcendentals=0
        ),
    )(*operands)


def sum_kernel(n_steps, n_parts, here_ref, *refs):
    out_ref = refs[-1]

    def add(own_ref, *received):
        scales = []
        for part in received:
            code = part[0, 0, pl.ds(STEP * BS, TAIL), :].astype(jnp.int32).astype(jnp.float32)
            scales.append(jnp.exp2(code * (1.0 / 16.0)) * (1.0 / QMAX))
        for r in range(STEP):
            at = slice(r * BS, (r + 1) * BS)
            total = own_ref[at, :]
            for part, scale in zip(received, scales):
                total = total + part[0, 0, at, :].astype(jnp.int32).astype(jnp.float32) * scale[r : r + 1, :]
            out_ref[at, :] = total.astype(jnp.bfloat16)

    for n in range(n_parts):
        pl.when(pl.program_id(0) // n_steps == n)(functools.partial(add, *refs[4 * n : 4 * n + 4]))


def summed(here, parts, rows, classes):
    block = STEP * BS
    n_steps = rows // STEP
    specs, operands = [], []
    for n, (own, received) in enumerate(parts):

        def at(g, n=n):
            return jnp.clip(g - n * n_steps, 0, n_steps - 1)

        specs.append(pl.BlockSpec((block, BS), lambda g, h, at=at: (at(g), 0)))
        for d in (1, 2, 3):
            specs.append(
                pl.BlockSpec(
                    (1, 1, block + TAIL, BS), lambda g, h, at=at, d=d: (lax.rem(h[0] + d, classes), at(g), 0, 0)
                )
            )
        operands += [own, received, received, received]
    grid_spec = pltpu.PrefetchScalarGridSpec(
        num_scalar_prefetch=1,
        grid=(len(parts) * n_steps,),
        in_specs=specs,
        out_specs=pl.BlockSpec((block, BS), lambda g, h: (g, 0)),
    )
    return pl.pallas_call(
        functools.partial(sum_kernel, n_steps, len(parts)),
        grid_spec=grid_spec,
        out_shape=jax.ShapeDtypeStruct((len(parts) * rows * BS, BS), jnp.bfloat16),
        compiler_params=pltpu.CompilerParams(vmem_limit_bytes=12 * 2**20),
    )(here, *operands)


def own_payload_kernel(half_rows, cols_ref, blocks_ref, out_ref, line_ref, sems):
    span = half_rows * BS
    cols_copy = pltpu.make_async_copy(cols_ref, line_ref, sems.at[2])
    cols_copy.start()
    copies = []
    for half in range(2):
        source, target = blocks_ref.at[pl.ds(half * span, span)], out_ref.at[half, pl.ds(0, span)]
        copies.append(pltpu.make_async_copy(source, target, sems.at[half]))
        copies[-1].start()
    rows = cols_ref.shape[1]
    cols_copy.wait()
    numbers = jnp.broadcast_to(line_ref[...].astype(jnp.float32), (TAIL, rows)).astype(jnp.bfloat16)
    for half in range(2):
        out_ref[half, pl.ds(span, TAIL), :] = jnp.zeros((TAIL, BS), jnp.bfloat16)
        out_ref[half, pl.ds(span, TAIL), pl.ds(0, rows)] = numbers
    for copy in copies:
        copy.wait()


def own_payload(blocks, cols, half_rows):
    return pl.pallas_call(
        functools.partial(own_payload_kernel, half_rows),
        in_specs=[pl.BlockSpec(memory_space=pl.ANY)] * 2,
        out_shape=jax.ShapeDtypeStruct((2, half_rows * BS + TAIL, BS), jnp.bfloat16),
        scratch_shapes=[pltpu.VMEM(cols.shape, cols.dtype), pltpu.SemaphoreType.DMA((3,))],
        compiler_params=pltpu.CompilerParams(vmem_limit_bytes=8 * 2**20),
    )(cols, blocks)


def pieces_kernel(classes, payload_ref, out_ref):
    rows = 2 * (payload_ref.shape[1] - TAIL) // BS
    for x in range(classes):
        for n in range(rows // classes):
            row = n * classes + x
            half, at = row // (rows // 2), row % (rows // 2) * BS
            block = payload_ref[half, pl.ds(at, BS), :]
            out_ref[x, pl.ds(n * BS, BS), :] = block
            out_ref[x + classes, pl.ds(n * BS, BS), :] = block
        tail = payload_ref[0, pl.ds(rows // 2 * BS, TAIL), :]
        out_ref[x, pl.ds(4 * BS, TAIL), :] = tail
        out_ref[x + classes, pl.ds(4 * BS, TAIL), :] = tail


def residue_pieces(payload, classes):
    return pl.pallas_call(
        functools.partial(pieces_kernel, classes),
        out_shape=jax.ShapeDtypeStruct((2 * classes, SPAN, BS), jnp.bfloat16),
        compiler_params=pltpu.CompilerParams(vmem_limit_bytes=8 * 2**20),
    )(payload)


def shards(p_blocks, p_cols):
    rows = p_blocks.shape[0]
    classes = lax.axis_size("depth")
    n_panels = lax.axis_size("row")
    matrix_rows = rows * n_panels
    r = lax.axis_index("row")
    core = lax.rem(r, 2)
    here = jnp.stack([lax.axis_index("depth"), core, (r - PANELS // 2) * rows]).astype(jnp.int32)

    blocks = pltpu.with_memory_space_constraint(p_blocks.reshape(rows * BS, BS), pltpu.HBM)
    cols = pltpu.with_memory_space_constraint(p_cols.reshape(1, rows), pltpu.HBM)
    own = own_payload(blocks, cols, rows // 2)
    down = up = own
    left = [own]
    for hop in range(3):
        down = passed_along(down, "col", 1)
        up = passed_along(up, "col", -1)
        left += [down, up]
        if hop == 0:
            after_first = (down, up)
    halves = [passed_along(down[0], "col", 1), passed_along(up[1], "col", -1)]

    pieces = residue_pieces(own, classes)
    groups = [[(2 * z + c) * classes + x for c in range(2) for x in range(classes)] for z in range(n_panels // 2)]
    pair = lax.all_to_all(pieces, ("row", "depth"), 0, 0, axis_index_groups=groups)
    pair = pair.reshape(2 * classes * SPAN, BS)
    pair, *_ = lax.optimization_barrier((pair,) + after_first)
    far = lax.ppermute(pair, "row", [(i, (i + (2 if i % 2 == 0 else -2)) % n_panels) for i in range(n_panels)])
    panel = classes * SPAN
    cross = jnp.where(core == 0, pair[:panel], pair[panel:])
    cross = lax.ppermute(cross, "row", [(i, (i + (-2 if i % 2 == 0 else 2)) % n_panels) for i in range(n_panels)])

    windows = (pair, far, cross)
    left[1:7] = [pltpu.with_memory_space_constraint(shard, pltpu.HBM) for shard in left[1:7]]
    idx, parts = None, []
    for start in range(0, rows, PART_ROWS):
        coded, mine, *found = products(
            here, idx, left + halves, windows, start, PART_ROWS, rows // 2, classes, matrix_rows
        )
        idx = found[0] if found else idx
        parts.append((mine, lax.all_to_all(coded, "depth", 0, 0)))
    return summed(here, parts, PART_ROWS, classes).reshape(rows, 1, BS, BS)


def solution(mesh):
    return jax.shard_map(
        shards,
        mesh=mesh,
        in_specs=(P("row", ("col", "depth"), None, None), P("row", ("col", "depth"))),
        out_specs=P("row", ("col", "depth"), None, None),
        check_vma=False,
    )
```

```python
import functools

import jax
import jax.numpy as jnp
from jax import lax
from jax.experimental import pallas as pl
from jax.experimental.pallas import tpu as pltpu
from jax.sharding import PartitionSpec as P

BS = 128
TAIL = 16
STEP = 8
PART_ROWS = 16
PANELS = 5
SPAN = 4 * BS + TAIL
QMAX = 32700.0
TINY = 2.0**-111


def passed_along(block, axis, distance):
    n = lax.axis_size(axis)
    return lax.ppermute(block, axis, [(i, (i + distance) % n) for i in range(n)])


def offsets(left_tails, window_tails, x, anchor, matrix_rows, classes, zero_at):
    sub = lax.broadcasted_iota(jnp.int32, (8, BS), 0)
    lane = lax.broadcasted_iota(jnp.int32, (8, BS), 1)

    def numbers(tile):
        return tile.astype(jnp.float32)[:8].astype(jnp.int32)

    cols = jnp.zeros((8, BS), jnp.int32)
    for s in range(8):
        cols = jnp.where(sub == s, numbers(left_tails[s]), cols)
    place = lax.shift_right_logical((cols - anchor + 2 * matrix_rows) & (matrix_rows - 1), 2)
    base = lax.shift_right_logical(place, 2) * (classes * SPAN) + (place & 3) * BS
    result = []
    for m in range(classes):
        tails = [numbers(window_tails[p * classes + m]) for p in range(PANELS)]
        found = jnp.zeros((8, BS), jnp.int32)
        for p in range(PANELS):
            for a in range(4):
                column = jnp.sum(jnp.where(lane == 4 * a + x, tails[p], 0), axis=1, keepdims=True)
                hit = (place == 4 * p + a) & (tails[PANELS // 2] == column)
                found = jnp.where(hit, 1, found)
        result.append(jnp.where(found == 1, base + m * SPAN, zero_at))
    return result


def product_kernel(first, start, half_rows, classes, matrix_rows, here_ref, *refs):
    if first:
        lefts, tail_sources, refs = refs[:9], refs[9:17], refs[17:]
        window_pieces, (pair, far, cross), refs = refs[:3], refs[3:6], refs[6:]
        q_ref, own_ref, wide, held, tails, idx_ref, sems = refs
    else:
        idx_ref, *refs = refs
        lefts, (pair, far, cross), refs = refs[:9], refs[9:12], refs[12:]
        q_ref, own_ref, held, sems = refs
    step = pl.program_id(0)
    panel = classes * SPAN
    zero_at = PANELS * panel
    x, core, anchor = here_ref[0], here_ref[1], here_ref[2]

    @pl.when(step == 0)
    def _():
        pieces = ((pair, 2 - core, 2), (far, 3 * core, 2), (cross, 4 - 4 * core, 1))
        copies, tail_copies = [], []
        if first:
            for s in range(8):
                at = pl.ds(half_rows * BS, TAIL)
                source = tail_sources[s].at[0, at] if s < 7 else tail_sources[s].at[at]
                tail_copies.append(pltpu.make_async_copy(source, tails.at[s], sems.at[s]))
            for n, (source, p, count) in enumerate(pieces):
                source = window_pieces[n].at[:, pl.ds(4 * BS, TAIL)]
                at = pl.ds(8 + p * classes, count * classes)
                tail_copies.append(pltpu.make_async_copy(source, tails.at[at], sems.at[8 + n]))
        for n, (source, p, count) in enumerate(pieces):
            at = pl.ds(pl.multiple_of(p * panel, TAIL), count * panel)
            copies.append(pltpu.make_async_copy(source, held.at[at], sems.at[11 + n]))
        for copy in copies + tail_copies:
            copy.start()
        held[pl.ds(zero_at, BS), :] = jnp.zeros((BS, BS), held.dtype)
        for copy in tail_copies:
            copy.wait()
        if first:
            left_tails = [tails[s] for s in range(8)]
            window_tails = [tails[8 + n] for n in range(PANELS * classes)]
            found = offsets(left_tails, window_tails, x, anchor, matrix_rows, classes, zero_at)
            for m in range(classes):
                wide[pl.ds(m * 8, 8), :] = found[m]
            copies.append(pltpu.make_async_copy(wide, idx_ref, sems.at[14]))
            copies[-1].start()
        for copy in copies:
            copy.wait()

    slots = [lax.rem(x + d, classes) for d in range(classes)]
    codes = [[] for _ in range(classes)]
    in_first_half = step * STEP + start < half_rows
    for r in range(STEP):
        at = slice(r * BS, (r + 1) * BS)
        row = step * STEP + r + start
        left = [ref[0, at, :] for ref in lefts[:7]]
        left.append(jnp.where(in_first_half, lefts[7][at, :], lefts[8][at, :]))
        left = jnp.concatenate(left, axis=1)
        right = []
        for d in range(classes):
            picked = []
            for s in range(8):
                k = idx_ref[slots[d] * 8 + s, row]
                picked.append(held[pl.ds(pl.multiple_of(k, TAIL), BS), :])
            right.append(jnp.concatenate(picked, axis=0))
        right = jnp.concatenate(right, axis=1)
        sums = jnp.dot(left, right, preferred_element_type=jnp.float32)
        own_ref[at, :] = sums[:, :BS]
        for d in range(1, classes):
            part = sums[:, d * BS : (d + 1) * BS]
            top = jnp.max(jnp.max(jnp.abs(part), axis=0, keepdims=True), axis=1, keepdims=True)
            code = jnp.ceil(jnp.log2(jnp.maximum(top, TINY)) * 16.0)
            scaled = part * (jnp.exp2(code * (-1.0 / 16.0)) * QMAX)
            coded = jnp.round(scaled).astype(jnp.int32)
            q_ref[slots[d], 0, at, :] = coded.astype(jnp.int16)
            codes[d].append(code)
    sub = lax.broadcasted_iota(jnp.int32, (TAIL, BS), 0)
    for d in range(1, classes):
        lines = jnp.zeros((TAIL, BS), jnp.float32)
        for r in range(STEP):
            lines = jnp.where(sub == r, codes[d][r], lines)
        q_ref[slots[d], 0, pl.ds(STEP * BS, TAIL), :] = lines.astype(jnp.int32).astype(jnp.int16)


def products(here, idx, lefts, windows, start, rows, half_rows, classes, matrix_rows):
    first = idx is None
    n_steps = rows // STEP
    per_half = half_rows // STEP
    block = STEP * BS
    anywhere = pl.BlockSpec(memory_space=pl.ANY)

    def left_at(g, *_):
        g = g + start // STEP
        return (g // per_half, g % per_half, 0)

    out_specs = [
        pl.BlockSpec((classes, 1, block + TAIL, BS), lambda g, *_: (0, g, 0, 0)),
        pl.BlockSpec((block, BS), lambda g, *_: (g, 0)),
    ]
    out_shape = [
        jax.ShapeDtypeStruct((classes, n_steps, block + TAIL, BS), jnp.int16),
        jax.ShapeDtypeStruct((rows * BS, BS), jnp.float32),
    ]
    scratch = [pltpu.VMEM((PANELS * classes * SPAN + BS, BS), jnp.bfloat16)]
    if first:
        out_specs.append(pl.BlockSpec((classes * 8, BS), lambda g, *_: (0, 0)))
        out_shape.append(jax.ShapeDtypeStruct((classes * 8, BS), jnp.int32))
        scratch += [pltpu.VMEM((8 + PANELS * classes, TAIL, BS), jnp.bfloat16), pltpu.SMEM((classes * 8, BS), jnp.int32)]
        operands = [here, *lefts, *lefts[:8], *(w.reshape(-1, SPAN, BS) for w in windows), *windows]
    else:
        operands = [here, idx, *lefts, *windows]
    grid_spec = pltpu.PrefetchScalarGridSpec(
        num_scalar_prefetch=1 if first else 2,
        grid=(n_steps,),
        in_specs=[pl.BlockSpec((1, block, BS), left_at)] * 7
        + [pl.BlockSpec((block, BS), lambda g, *_: (jnp.minimum(g + start // STEP, per_half - 1), 0))]
        + [pl.BlockSpec((block, BS), lambda g, *_: (jnp.maximum(g + start // STEP - per_half, 0), 0))]
        + [anywhere] * (14 if first else 3),
        out_specs=out_specs,
        scratch_shapes=scratch + [pltpu.SemaphoreType.DMA((15,))],
    )
    return pl.pallas_call(
        functools.partial(product_kernel, first, start, half_rows, classes, matrix_rows),
        grid_spec=grid_spec,
        out_shape=out_shape,
        compiler_params=pltpu.CompilerParams(vmem_limit_bytes=20 * 2**20),
        cost_estimate=pl.CostEstimate(
            flops=2 * rows * 32 * BS**3, bytes_accessed=12 * 2**20, transcendentals=0
        ),
    )(*operands)


def sum_kernel(n_steps, n_parts, here_ref, *refs):
    out_ref = refs[-1]

    def add(own_ref, *received):
        scales = []
        for part in received:
            code = part[0, 0, pl.ds(STEP * BS, TAIL), :].astype(jnp.int32).astype(jnp.float32)
            scales.append(jnp.exp2(code * (1.0 / 16.0)) * (1.0 / QMAX))
        for r in range(STEP):
            at = slice(r * BS, (r + 1) * BS)
            total = own_ref[at, :]
            for part, scale in zip(received, scales):
                total = total + part[0, 0, at, :].astype(jnp.int32).astype(jnp.float32) * scale[r : r + 1, :]
            out_ref[at, :] = total.astype(jnp.bfloat16)

    for n in range(n_parts):
        pl.when(pl.program_id(0) // n_steps == n)(functools.partial(add, *refs[4 * n : 4 * n + 4]))


def summed(here, parts, rows, classes):
    block = STEP * BS
    n_steps = rows // STEP
    specs, operands = [], []
    for n, (own, received) in enumerate(parts):

        def at(g, n=n):
            return jnp.clip(g - n * n_steps, 0, n_steps - 1)

        specs.append(pl.BlockSpec((block, BS), lambda g, h, at=at: (at(g), 0)))
        for d in (1, 2, 3):
            specs.append(
                pl.BlockSpec(
                    (1, 1, block + TAIL, BS), lambda g, h, at=at, d=d: (lax.rem(h[0] + d, classes), at(g), 0, 0)
                )
            )
        operands += [own, received, received, received]
    grid_spec = pltpu.PrefetchScalarGridSpec(
        num_scalar_prefetch=1,
        grid=(len(parts) * n_steps,),
        in_specs=specs,
        out_specs=pl.BlockSpec((block, BS), lambda g, h: (g, 0)),
    )
    return pl.pallas_call(
        functools.partial(sum_kernel, n_steps, len(parts)),
        grid_spec=grid_spec,
        out_shape=jax.ShapeDtypeStruct((len(parts) * rows * BS, BS), jnp.bfloat16),
        compiler_params=pltpu.CompilerParams(vmem_limit_bytes=12 * 2**20),
    )(here, *operands)


def own_payload_kernel(half_rows, cols_ref, blocks_ref, out_ref, line_ref, sems):
    span = half_rows * BS
    cols_copy = pltpu.make_async_copy(cols_ref, line_ref, sems.at[2])
    cols_copy.start()
    copies = []
    for half in range(2):
        source, target = blocks_ref.at[pl.ds(half * span, span)], out_ref.at[half, pl.ds(0, span)]
        copies.append(pltpu.make_async_copy(source, target, sems.at[half]))
        copies[-1].start()
    rows = cols_ref.shape[1]
    cols_copy.wait()
    numbers = jnp.broadcast_to(line_ref[...].astype(jnp.float32), (TAIL, rows)).astype(jnp.bfloat16)
    for half in range(2):
        out_ref[half, pl.ds(span, TAIL), :] = jnp.zeros((TAIL, BS), jnp.bfloat16)
        out_ref[half, pl.ds(span, TAIL), pl.ds(0, rows)] = numbers
    for copy in copies:
        copy.wait()


def own_payload(blocks, cols, half_rows):
    return pl.pallas_call(
        functools.partial(own_payload_kernel, half_rows),
        in_specs=[pl.BlockSpec(memory_space=pl.ANY)] * 2,
        out_shape=jax.ShapeDtypeStruct((2, half_rows * BS + TAIL, BS), jnp.bfloat16),
        scratch_shapes=[pltpu.VMEM(cols.shape, cols.dtype), pltpu.SemaphoreType.DMA((3,))],
        compiler_params=pltpu.CompilerParams(vmem_limit_bytes=8 * 2**20),
    )(cols, blocks)


def pieces_kernel(classes, payload_ref, out_ref):
    rows = 2 * (payload_ref.shape[1] - TAIL) // BS
    for x in range(classes):
        for n in range(rows // classes):
            row = n * classes + x
            half, at = row // (rows // 2), row % (rows // 2) * BS
            block = payload_ref[half, pl.ds(at, BS), :]
            out_ref[x, pl.ds(n * BS, BS), :] = block
            out_ref[x + classes, pl.ds(n * BS, BS), :] = block
        tail = payload_ref[0, pl.ds(rows // 2 * BS, TAIL), :]
        out_ref[x, pl.ds(4 * BS, TAIL), :] = tail
        out_ref[x + classes, pl.ds(4 * BS, TAIL), :] = tail


def residue_pieces(payload, classes):
    return pl.pallas_call(
        functools.partial(pieces_kernel, classes),
        out_shape=jax.ShapeDtypeStruct((2 * classes, SPAN, BS), jnp.bfloat16),
        compiler_params=pltpu.CompilerParams(vmem_limit_bytes=8 * 2**20),
    )(payload)


def shards(p_blocks, p_cols):
    rows = p_blocks.shape[0]
    classes = lax.axis_size("depth")
    n_panels = lax.axis_size("row")
    matrix_rows = rows * n_panels
    r = lax.axis_index("row")
    core = lax.rem(r, 2)
    here = jnp.stack([lax.axis_index("depth"), core, (r - PANELS // 2) * rows]).astype(jnp.int32)

    blocks = pltpu.with_memory_space_constraint(p_blocks.reshape(rows * BS, BS), pltpu.HBM)
    cols = pltpu.with_memory_space_constraint(p_cols.reshape(1, rows), pltpu.HBM)
    own = own_payload(blocks, cols, rows // 2)
    down = up = own
    left = [own]
    for hop in range(3):
        down = passed_along(down, "col", 1)
        up = passed_along(up, "col", -1)
        left += [down, up]
        if hop == 0:
            after_first = (down, up)
    halves = [passed_along(down[0], "col", 1), passed_along(up[1], "col", -1)]

    pieces = residue_pieces(own, classes)
    groups = [[(2 * z + c) * classes + x for c in range(2) for x in range(classes)] for z in range(n_panels // 2)]
    pair = lax.all_to_all(pieces, ("row", "depth"), 0, 0, axis_index_groups=groups)
    pair = pair.reshape(2 * classes * SPAN, BS)
    pair, *_ = lax.optimization_barrier((pair,) + after_first)
    far = lax.ppermute(pair, "row", [(i, (i + (2 if i % 2 == 0 else -2)) % n_panels) for i in range(n_panels)])
    panel = classes * SPAN
    cross = jnp.where(core == 0, pair[:panel], pair[panel:])
    cross = lax.ppermute(cross, "row", [(i, (i + (-2 if i % 2 == 0 else 2)) % n_panels) for i in range(n_panels)])

    windows = (pair, far, cross)
    left[1:7] = [pltpu.with_memory_space_constraint(shard, pltpu.HBM) for shard in left[1:7]]
    idx, parts = None, []
    for start in range(0, rows, PART_ROWS):
        coded, mine, *found = products(
            here, idx, left + halves, windows, start, PART_ROWS, rows // 2, classes, matrix_rows
        )
        idx = found[0] if found else idx
        parts.append((mine, lax.all_to_all(coded, "depth", 0, 0)))
    return summed(here, parts, PART_ROWS, classes).reshape(rows, 1, BS, BS)


def solution(mesh):
    return jax.shard_map(
        shards,
        mesh=mesh,
        in_specs=(P("row", ("col", "depth"), None, None), P("row", ("col", "depth"))),
        out_specs=P("row", ("col", "depth"), None, None),
        check_vma=False,
    )
```

```python
import functools

import jax
import jax.numpy as jnp
from jax import lax
from jax.experimental import pallas as pl
from jax.experimental.pallas import tpu as pltpu
from jax.sharding import PartitionSpec as P

BS = 128
TAIL = 16
STEP = 8
PART_ROWS = 16
PANELS = 5
SPAN = 4 * BS + TAIL
QMAX = 32700.0
TINY = 2.0**-111


def passed_along(block, axis, distance):
    n = lax.axis_size(axis)
    return lax.ppermute(block, axis, [(i, (i + distance) % n) for i in range(n)])


def offsets(left_tails, window_tails, x, anchor, matrix_rows, classes, zero_at):
    sub = lax.broadcasted_iota(jnp.int32, (8, BS), 0)
    lane = lax.broadcasted_iota(jnp.int32, (8, BS), 1)

    def numbers(tile):
        return tile.astype(jnp.float32)[:8].astype(jnp.int32)

    cols = jnp.zeros((8, BS), jnp.int32)
    for s in range(8):
        cols = jnp.where(sub == s, numbers(left_tails[s]), cols)
    place = lax.shift_right_logical((cols - anchor + 2 * matrix_rows) & (matrix_rows - 1), 2)
    base = lax.shift_right_logical(place, 2) * (classes * SPAN) + (place & 3) * BS
    result = []
    for m in range(classes):
        tails = [numbers(window_tails[p * classes + m]) for p in range(PANELS)]
        found = jnp.zeros((8, BS), jnp.int32)
        for p in range(PANELS):
            for a in range(4):
                column = jnp.sum(jnp.where(lane == 4 * a + x, tails[p], 0), axis=1, keepdims=True)
                hit = (place == 4 * p + a) & (tails[PANELS // 2] == column)
                found = jnp.where(hit, 1, found)
        result.append(jnp.where(found == 1, base + m * SPAN, zero_at))
    return result


def product_kernel(first, start, half_rows, classes, matrix_rows, here_ref, *refs):
    if first:
        lefts, tail_sources, refs = refs[:9], refs[9:17], refs[17:]
        window_pieces, (pair, far, cross), refs = refs[:3], refs[3:6], refs[6:]
        q_ref, own_ref, wide, held, tails, idx_ref, sems = refs
    else:
        idx_ref, *refs = refs
        lefts, (pair, far, cross), refs = refs[:9], refs[9:12], refs[12:]
        q_ref, own_ref, held, sems = refs
    step = pl.program_id(0)
    panel = classes * SPAN
    zero_at = PANELS * panel
    x, core, anchor = here_ref[0], here_ref[1], here_ref[2]

    @pl.when(step == 0)
    def _():
        pieces = ((pair, 2 - core, 2), (far, 3 * core, 2), (cross, 4 - 4 * core, 1))
        copies, tail_copies = [], []
        if first:
            for s in range(8):
                at = pl.ds(half_rows * BS, TAIL)
                source = tail_sources[s].at[0, at] if s < 7 else tail_sources[s].at[at]
                tail_copies.append(pltpu.make_async_copy(source, tails.at[s], sems.at[s]))
            for n, (source, p, count) in enumerate(pieces):
                source = window_pieces[n].at[:, pl.ds(4 * BS, TAIL)]
                at = pl.ds(8 + p * classes, count * classes)
                tail_copies.append(pltpu.make_async_copy(source, tails.at[at], sems.at[8 + n]))
        for n, (source, p, count) in enumerate(pieces):
            at = pl.ds(pl.multiple_of(p * panel, TAIL), count * panel)
            copies.append(pltpu.make_async_copy(source, held.at[at], sems.at[11 + n]))
        for copy in tail_copies + copies:
            copy.start()
        held[pl.ds(zero_at, BS), :] = jnp.zeros((BS, BS), held.dtype)
        for copy in tail_copies:
            copy.wait()
        if first:
            left_tails = [tails[s] for s in range(8)]
            window_tails = [tails[8 + n] for n in range(PANELS * classes)]
            found = offsets(left_tails, window_tails, x, anchor, matrix_rows, classes, zero_at)
            for m in range(classes):
                wide[pl.ds(m * 8, 8), :] = found[m]
            copies.append(pltpu.make_async_copy(wide, idx_ref, sems.at[14]))
            copies[-1].start()
        for copy in copies:
            copy.wait()

    slots = [lax.rem(x + d, classes) for d in range(classes)]
    codes = [[] for _ in range(classes)]
    in_first_half = step * STEP + start < half_rows
    for r in range(STEP):
        at = slice(r * BS, (r + 1) * BS)
        row = step * STEP + r + start
        left = [ref[0, at, :] for ref in lefts[:7]]
        left.append(jnp.where(in_first_half, lefts[7][at, :], lefts[8][at, :]))
        left = jnp.concatenate(left, axis=1)
        right = []
        for d in range(classes):
            picked = []
            for s in range(8):
                k = idx_ref[slots[d] * 8 + s, row]
                picked.append(held[pl.ds(pl.multiple_of(k, TAIL), BS), :])
            right.append(jnp.concatenate(picked, axis=0))
        right = jnp.concatenate(right, axis=1)
        sums = jnp.dot(left, right, preferred_element_type=jnp.float32)
        own_ref[at, :] = sums[:, :BS]
        for d in range(1, classes):
            part = sums[:, d * BS : (d + 1) * BS]
            top = jnp.max(jnp.max(jnp.abs(part), axis=0, keepdims=True), axis=1, keepdims=True)
            code = jnp.ceil(jnp.log2(jnp.maximum(top, TINY)) * 16.0)
            scaled = part * (jnp.exp2(code * (-1.0 / 16.0)) * QMAX)
            coded = jnp.round(scaled).astype(jnp.int32)
            q_ref[slots[d], 0, at, :] = coded.astype(jnp.int16)
            codes[d].append(code)
    sub = lax.broadcasted_iota(jnp.int32, (TAIL, BS), 0)
    for d in range(1, classes):
        lines = jnp.zeros((TAIL, BS), jnp.float32)
        for r in range(STEP):
            lines = jnp.where(sub == r, codes[d][r], lines)
        q_ref[slots[d], 0, pl.ds(STEP * BS, TAIL), :] = lines.astype(jnp.int32).astype(jnp.int16)


def products(here, idx, lefts, windows, start, rows, half_rows, classes, matrix_rows):
    first = idx is None
    n_steps = rows // STEP
    per_half = half_rows // STEP
    block = STEP * BS
    anywhere = pl.BlockSpec(memory_space=pl.ANY)

    def left_at(g, *_):
        g = g + start // STEP
        return (g // per_half, g % per_half, 0)

    out_specs = [
        pl.BlockSpec((classes, 1, block + TAIL, BS), lambda g, *_: (0, g, 0, 0)),
        pl.BlockSpec((block, BS), lambda g, *_: (g, 0)),
    ]
    out_shape = [
        jax.ShapeDtypeStruct((classes, n_steps, block + TAIL, BS), jnp.int16),
        jax.ShapeDtypeStruct((rows * BS, BS), jnp.float32),
    ]
    scratch = [pltpu.VMEM((PANELS * classes * SPAN + BS, BS), jnp.bfloat16)]
    if first:
        out_specs.append(pl.BlockSpec((classes * 8, BS), lambda g, *_: (0, 0)))
        out_shape.append(jax.ShapeDtypeStruct((classes * 8, BS), jnp.int32))
        scratch += [pltpu.VMEM((8 + PANELS * classes, TAIL, BS), jnp.bfloat16), pltpu.SMEM((classes * 8, BS), jnp.int32)]
        operands = [here, *lefts, *lefts[:8], *(w.reshape(-1, SPAN, BS) for w in windows), *windows]
    else:
        operands = [here, idx, *lefts, *windows]
    grid_spec = pltpu.PrefetchScalarGridSpec(
        num_scalar_prefetch=1 if first else 2,
        grid=(n_steps,),
        in_specs=[pl.BlockSpec((1, block, BS), left_at)] * 7
        + [pl.BlockSpec((block, BS), lambda g, *_: (jnp.minimum(g + start // STEP, per_half - 1), 0))]
        + [pl.BlockSpec((block, BS), lambda g, *_: (jnp.maximum(g + start // STEP - per_half, 0), 0))]
        + [anywhere] * (14 if first else 3),
        out_specs=out_specs,
        scratch_shapes=scratch + [pltpu.SemaphoreType.DMA((15,))],
    )
    return pl.pallas_call(
        functools.partial(product_kernel, first, start, half_rows, classes, matrix_rows),
        grid_spec=grid_spec,
        out_shape=out_shape,
        compiler_params=pltpu.CompilerParams(vmem_limit_bytes=14 * 2**20),
        cost_estimate=pl.CostEstimate(
            flops=2 * rows * 32 * BS**3, bytes_accessed=12 * 2**20, transcendentals=0
        ),
    )(*operands)


def sum_kernel(n_steps, n_parts, here_ref, *refs):
    out_ref = refs[-1]

    def add(own_ref, *received):
        scales = []
        for part in received:
            code = part[0, 0, pl.ds(STEP * BS, TAIL), :].astype(jnp.int32).astype(jnp.float32)
            scales.append(jnp.exp2(code * (1.0 / 16.0)) * (1.0 / QMAX))
        for r in range(STEP):
            at = slice(r * BS, (r + 1) * BS)
            total = own_ref[at, :]
            for part, scale in zip(received, scales):
                total = total + part[0, 0, at, :].astype(jnp.int32).astype(jnp.float32) * scale[r : r + 1, :]
            out_ref[at, :] = total.astype(jnp.bfloat16)

    for n in range(n_parts):
        pl.when(pl.program_id(0) // n_steps == n)(functools.partial(add, *refs[4 * n : 4 * n + 4]))


def summed(here, parts, rows, classes):
    block = STEP * BS
    n_steps = rows // STEP
    specs, operands = [], []
    for n, (own, received) in enumerate(parts):

        def at(g, n=n):
            return jnp.clip(g - n * n_steps, 0, n_steps - 1)

        specs.append(pl.BlockSpec((block, BS), lambda g, h, at=at: (at(g), 0)))
        for d in (1, 2, 3):
            specs.append(
                pl.BlockSpec(
                    (1, 1, block + TAIL, BS), lambda g, h, at=at, d=d: (lax.rem(h[0] + d, classes), at(g), 0, 0)
                )
            )
        operands += [own, received, received, received]
    grid_spec = pltpu.PrefetchScalarGridSpec(
        num_scalar_prefetch=1,
        grid=(len(parts) * n_steps,),
        in_specs=specs,
        out_specs=pl.BlockSpec((block, BS), lambda g, h: (g, 0)),
    )
    return pl.pallas_call(
        functools.partial(sum_kernel, n_steps, len(parts)),
        grid_spec=grid_spec,
        out_shape=jax.ShapeDtypeStruct((len(parts) * rows * BS, BS), jnp.bfloat16),
        compiler_params=pltpu.CompilerParams(vmem_limit_bytes=12 * 2**20),
    )(here, *operands)


def own_payload_kernel(half_rows, cols_ref, blocks_ref, out_ref, line_ref, sems):
    span = half_rows * BS
    cols_copy = pltpu.make_async_copy(cols_ref, line_ref, sems.at[2])
    cols_copy.start()
    copies = []
    for half in range(2):
        source, target = blocks_ref.at[pl.ds(half * span, span)], out_ref.at[half, pl.ds(0, span)]
        copies.append(pltpu.make_async_copy(source, target, sems.at[half]))
        copies[-1].start()
    rows = cols_ref.shape[1]
    cols_copy.wait()
    numbers = jnp.broadcast_to(line_ref[...].astype(jnp.float32), (TAIL, rows)).astype(jnp.bfloat16)
    for half in range(2):
        out_ref[half, pl.ds(span, TAIL), :] = jnp.zeros((TAIL, BS), jnp.bfloat16)
        out_ref[half, pl.ds(span, TAIL), pl.ds(0, rows)] = numbers
    for copy in copies:
        copy.wait()


def own_payload(blocks, cols, half_rows):
    return pl.pallas_call(
        functools.partial(own_payload_kernel, half_rows),
        in_specs=[pl.BlockSpec(memory_space=pl.ANY)] * 2,
        out_shape=jax.ShapeDtypeStruct((2, half_rows * BS + TAIL, BS), jnp.bfloat16),
        scratch_shapes=[pltpu.VMEM(cols.shape, cols.dtype), pltpu.SemaphoreType.DMA((3,))],
        compiler_params=pltpu.CompilerParams(vmem_limit_bytes=8 * 2**20),
    )(cols, blocks)


def pieces_kernel(classes, payload_ref, out_ref):
    rows = 2 * (payload_ref.shape[1] - TAIL) // BS
    for x in range(classes):
        for n in range(rows // classes):
            row = n * classes + x
            half, at = row // (rows // 2), row % (rows // 2) * BS
            block = payload_ref[half, pl.ds(at, BS), :]
            out_ref[x, pl.ds(n * BS, BS), :] = block
            out_ref[x + classes, pl.ds(n * BS, BS), :] = block
        tail = payload_ref[0, pl.ds(rows // 2 * BS, TAIL), :]
        out_ref[x, pl.ds(4 * BS, TAIL), :] = tail
        out_ref[x + classes, pl.ds(4 * BS, TAIL), :] = tail


def residue_pieces(payload, classes):
    return pl.pallas_call(
        functools.partial(pieces_kernel, classes),
        out_shape=jax.ShapeDtypeStruct((2 * classes, SPAN, BS), jnp.bfloat16),
        compiler_params=pltpu.CompilerParams(vmem_limit_bytes=8 * 2**20),
    )(payload)


def shards(p_blocks, p_cols):
    rows = p_blocks.shape[0]
    classes = lax.axis_size("depth")
    n_panels = lax.axis_size("row")
    matrix_rows = rows * n_panels
    r = lax.axis_index("row")
    core = lax.rem(r, 2)
    here = jnp.stack([lax.axis_index("depth"), core, (r - PANELS // 2) * rows]).astype(jnp.int32)

    blocks = pltpu.with_memory_space_constraint(p_blocks.reshape(rows * BS, BS), pltpu.HBM)
    cols = pltpu.with_memory_space_constraint(p_cols.reshape(1, rows), pltpu.HBM)
    own = own_payload(blocks, cols, rows // 2)
    down = up = own
    left = [own]
    for hop in range(3):
        down = passed_along(down, "col", 1)
        up = passed_along(up, "col", -1)
        left += [down, up]
        if hop == 0:
            after_first = (down, up)
    halves = [passed_along(down[0], "col", 1), passed_along(up[1], "col", -1)]

    pieces = residue_pieces(own, classes)
    groups = [[(2 * z + c) * classes + x for c in range(2) for x in range(classes)] for z in range(n_panels // 2)]
    pair = lax.all_to_all(pieces, ("row", "depth"), 0, 0, axis_index_groups=groups)
    pair = pair.reshape(2 * classes * SPAN, BS)
    pair, *_ = lax.optimization_barrier((pair,) + after_first)
    far = lax.ppermute(pair, "row", [(i, (i + (2 if i % 2 == 0 else -2)) % n_panels) for i in range(n_panels)])
    panel = classes * SPAN
    cross = jnp.where(core == 0, pair[:panel], pair[panel:])
    cross = lax.ppermute(cross, "row", [(i, (i + (-2 if i % 2 == 0 else 2)) % n_panels) for i in range(n_panels)])

    windows = (pair, far, cross)
    left[1:7] = [pltpu.with_memory_space_constraint(shard, pltpu.HBM) for shard in left[1:7]]
    idx, parts = None, []
    for start in range(0, rows, PART_ROWS):
        coded, mine, *found = products(
            here, idx, left + halves, windows, start, PART_ROWS, rows // 2, classes, matrix_rows
        )
        idx = found[0] if found else idx
        parts.append((mine, lax.all_to_all(coded, "depth", 0, 0)))
    return summed(here, parts, PART_ROWS, classes).reshape(rows, 1, BS, BS)


def solution(mesh):
    return jax.shard_map(
        shards,
        mesh=mesh,
        in_specs=(P("row", ("col", "depth"), None, None), P("row", ("col", "depth"))),
        out_specs=P("row", ("col", "depth"), None, None),
        check_vma=False,
    )
```
